512 devices in a mesh: tile: 64 (over z_hi, y, x), narrow: 8 (over z_lo, core).
Axes of the slice: x: 4, y: 4, z: 16 (z_hi: 4, z_lo: 4; z = z_hi * 4 + z_lo), core: 2. Of those that a mesh axis runs over, the one named last changes fastest.
Arguments:
- fine: bfloat16 [1024, 64, 512], P('tile', 'narrow'), may hold values from -6 to 6
- coarse: bfloat16 [256, 128, 1024], P('tile'), may hold values from -6 to 6
- block_table: int32 [64, 8], P('tile'), may hold values from 0 to 255, as said below
- shifts: int32 [2], replicated, may hold values from 1 to 7
- attn_gain: float32 [512], replicated, may hold values from 0.1 to 1.9
- w_query: bfloat16 [512, 512], replicated, may hold values from -8 to 8
- w_key: bfloat16 [512, 512], replicated, may hold values from -8 to 8
- w_value: bfloat16 [512, 512], replicated, may hold values from -0.25 to 0.25
- w_out: bfloat16 [512, 512], replicated, may hold values from -0.25 to 0.25
- coarse_key: bfloat16 [1024, 512], replicated, may hold values from -0.1875 to 0.1875
- coarse_value: bfloat16 [1024, 512], replicated, may hold values from -0.1875 to 0.1875
- mlp_gain: float32 [512], replicated, may hold values from 0.1 to 1.9
- w_gate: bfloat16 [512, 2048], replicated, may hold values from -0.25 to 0.25
- w_up: bfloat16 [512, 2048], replicated, may hold values from -0.25 to 0.25
- w_down: bfloat16 [2048, 512], replicated, may hold values from -0.125 to 0.125
Outputs:
- output: bfloat16 [1024, 64, 512], P('tile', 'narrow')
The draws below stay inside these ranges and needn't reach their ends.
Inputs may be any that keep to these rules, and one draw needn't show every extreme that they name: `block_table`: row s names 8 distinct blocks, all among blocks (s - 1) * 4 to (s + 2) * 4 - 1 taken modulo 256, at least one of them below s * 4 and at least one at or above (s + 1) * 4 in that range.
All inputs are finite; a program needn't handle non-finite values.
Results may differ from the reference program's by a relative error of at most 0.0073.
Values may be sent and summed in bfloat16 or wider, within the bound.
No kernel may reach another device: no remote copies, remote signals or barrier semaphores. Data moves between devices by JAX's collectives and lax.ppermute only.
A program may use at most 64 MiB of HBM per device.

```python
import jax
import jax.numpy as jnp
from jax import lax

FD = 512
HEADS = 8
CW = 1024
FF = 2048
WS = 8
SR = 16
CT = 128
CB_DEV = 4
NB = 8
HD = 64
SC = 64
STRIPS = 64
ROWS = 1024
CBLOCKS = 256


def draw_block_table(key, part):
    key = jax.random.fold_in(key, 11)
    span = 3 * CB_DEV
    position = jnp.arange(span, dtype=jnp.int32)[None, :]
    scores = jax.random.randint(jax.random.fold_in(key, 1), (STRIPS, span), 0, 1 << 20) * span + position
    lower_pick = jax.random.randint(jax.random.fold_in(key, 2), (STRIPS, 1), 0, CB_DEV)
    upper_pick = jax.random.randint(jax.random.fold_in(key, 3), (STRIPS, 1), 0, CB_DEV) + 2 * CB_DEV
    forced = (position == lower_pick) | (position == upper_pick)
    scores = jnp.where(forced, position - 2 * span, scores)
    order = jnp.argsort(scores, axis=1)[:, :NB].astype(jnp.int32)
    first = (jnp.arange(STRIPS, dtype=jnp.int32) - 1) * CB_DEV
    return jnp.mod(first[:, None] + order, CBLOCKS).astype(jnp.int32)


def draw_fine(key, part):
    key = jax.random.fold_in(key, 21)
    noise = jax.random.normal(jax.random.fold_in(key, 1), (ROWS, SC, FD), jnp.float32)
    return jnp.clip(noise, -6.0, 6.0).astype(jnp.bfloat16)


def draw_w_query(key, part):
    key = jax.random.fold_in(key, 31)
    matrix = jax.random.normal(key, (FD, FD), jnp.float32) * FD ** (-0.5)
    return jnp.clip(matrix, -8.0, 8.0).astype(jnp.bfloat16)


def draw_w_key(key, part):
    key = jax.random.fold_in(key, 41)
    matrix = jax.random.normal(key, (FD, FD), jnp.float32) * FD ** (-0.5)
    return jnp.clip(matrix, -8.0, 8.0).astype(jnp.bfloat16)


def block_levels(rng, extent, pieces, low, high):
    def one(dim, parts):
        draws = jax.random.uniform(jax.random.fold_in(jax.random.fold_in(rng, 6), dim), (parts,), jnp.float32, low / len(pieces), high / len(pieces))
        return jnp.repeat(jnp.exp(draws), extent[dim] // parts).reshape((-1,) + (1,) * (len(extent) - dim - 1))

    loudness = one(*pieces[0])
    for cut in pieces[1:]:
        loudness = loudness * one(*cut)
    return loudness


def gaussian(own_key, dims, scale, most, split=(), held_as=jnp.bfloat16):
    drawn = jax.random.normal(own_key, dims, jnp.float32) * scale
    if len(split) > 0:
        drawn = block_levels(own_key, dims, split, -0.22, 0.18) * drawn
    return jnp.clip(drawn, min=-most, max=most).astype(held_as)


def setup_inputs(seed: int = 0) -> dict:
    streams_of = jax.random.split(jax.random.key(seed), 16)
    fine = draw_fine(jax.random.fold_in(streams_of[15], 71), 0)
    coarse = gaussian(streams_of[1], (CBLOCKS, CT, CW), 1.0, 6.0, ((0, 64),))
    block_table = draw_block_table(jax.random.fold_in(streams_of[15], 71), 0)
    shifts = jax.random.randint(streams_of[3], (2,), 1, WS).astype(jnp.int32)
    attn_gain = jnp.clip(1.0 + 0.18 * jax.random.normal(streams_of[4], (FD,), jnp.float32), 0.1, 1.9)
    w_query = draw_w_query(jax.random.fold_in(streams_of[15], 71), 0)
    w_key = draw_w_key(jax.random.fold_in(streams_of[15], 71), 0)
    w_value = gaussian(streams_of[7], (FD, FD), FD ** -0.5, 0.25)
    w_out = gaussian(streams_of[8], (FD, FD), FD ** -0.5, 0.25)
    coarse_key = gaussian(streams_of[9], (CW, FD), CW ** -0.5, 0.1875)
    coarse_value = gaussian(streams_of[10], (CW, FD), CW ** -0.5, 0.1875)
    mlp_gain = jnp.clip(1.0 + 0.18 * jax.random.normal(streams_of[11], (FD,), jnp.float32), 0.1, 1.9)
    w_gate = gaussian(streams_of[12], (FD, FF), FD ** -0.5, 0.25)
    w_up = gaussian(streams_of[13], (FD, FF), FD ** -0.5, 0.25)
    w_down = gaussian(streams_of[14], (FF, FD), FF ** -0.5, 0.125)
    return {"fine": fine, "coarse": coarse, "block_table": block_table, "shifts": shifts, "attn_gain": attn_gain, "w_query": w_query, "w_key": w_key, "w_value": w_value, "w_out": w_out, "coarse_key": coarse_key, "coarse_value": coarse_value, "mlp_gain": mlp_gain, "w_gate": w_gate, "w_up": w_up, "w_down": w_down}


def rms_scale(source, gain_vec):
    values = source.astype(jnp.float32)
    mean_square = lax.optimization_barrier(jnp.mean(values * values, axis=-1, keepdims=True))
    return values * lax.rsqrt(mean_square + 1e-06) * gain_vec.astype(jnp.float32)

def to_windows(source):
    lead_count = source.shape[0] // WS
    across = source.shape[1] // WS
    reordered = source.reshape((lead_count, WS, across, WS) + source.shape[2:])
    reordered = jnp.swapaxes(reordered, 1, 2)
    return reordered.reshape((lead_count * across, WS * WS) + source.shape[2:])

def from_windows(source, row_count, column_count):
    reordered = source.reshape((row_count // WS, column_count // WS, WS, WS) + source.shape[2:])
    reordered = jnp.swapaxes(reordered, 1, 2)
    return reordered.reshape((row_count, column_count) + source.shape[2:])

def attend(queries, keys_fine, values_fine, coarse_keys, coarse_values, row_flag, column_flag):
    row_count, column_count = (queries.shape[0], queries.shape[1])
    labels = row_flag.astype(jnp.int32)[:, None] * 2 + column_flag.astype(jnp.int32)[None, :]
    labels = to_windows(labels)
    allowed = labels[:, :, None] == labels[:, None, :]
    query_win = to_windows(queries).astype(jnp.float32)
    key_win = to_windows(keys_fine).astype(jnp.float32)
    value_win = to_windows(values_fine).astype(jnp.float32)
    score_self = jnp.einsum('wqhd,wkhd->whqk', query_win, key_win)
    score_self = jnp.where(allowed[:, None], score_self, -jnp.inf)
    score_cross = jnp.einsum('wqhd,khd->whqk', query_win, coarse_keys.astype(jnp.float32))
    maxima = jnp.maximum(lax.optimization_barrier(jnp.max(score_self, axis=-1, keepdims=True)), lax.optimization_barrier(jnp.max(score_cross, axis=-1, keepdims=True)))
    exp_self = jnp.exp(score_self - maxima)
    exp_cross = jnp.exp(score_cross - maxima)
    totals = lax.optimization_barrier(jnp.sum(exp_self, axis=-1, keepdims=True)) + lax.optimization_barrier(jnp.sum(exp_cross, axis=-1, keepdims=True))
    prob_self = (exp_self / totals).astype(jnp.bfloat16).astype(jnp.float32)
    prob_cross = (exp_cross / totals).astype(jnp.bfloat16).astype(jnp.float32)
    mixture = jnp.einsum('whqk,wkhd->wqhd', prob_self, value_win)
    mixture = mixture + jnp.einsum('whqk,khd->wqhd', prob_cross, coarse_values.astype(jnp.float32))
    return from_windows(mixture.astype(jnp.bfloat16), row_count, column_count)

def reference(fine, coarse, block_table, shifts, attn_gain, w_query, w_key, w_value, w_out, coarse_key, coarse_value, mlp_gain, w_gate, w_up, w_down):
    shift_row = shifts[0]
    shift_col = shifts[1]
    row_total, column_count = (fine.shape[0], fine.shape[1])
    rolled = jnp.roll(fine, (-shift_row, -shift_col), axis=(0, 1))
    flat_rows = rolled.reshape(-1, FD)
    normed = rms_scale(flat_rows, attn_gain).astype(jnp.bfloat16)
    query_scale = 1.0 / HD ** 0.5
    queries = (jnp.dot(normed, w_query, preferred_element_type=jnp.float32) * query_scale).astype(jnp.bfloat16)
    keys_fine = jnp.dot(normed, w_key, preferred_element_type=jnp.float32).astype(jnp.bfloat16)
    values_fine = jnp.dot(normed, w_value, preferred_element_type=jnp.float32).astype(jnp.bfloat16)
    queries = queries.reshape(row_total, column_count, HEADS, HD)
    keys_fine = keys_fine.reshape(row_total, column_count, HEADS, HD)
    values_fine = values_fine.reshape(row_total, column_count, HEADS, HD)
    coarse_flat = coarse.reshape(-1, CW)
    coarse_keys = jnp.dot(coarse_flat, coarse_key, preferred_element_type=jnp.float32).astype(jnp.bfloat16).reshape(CBLOCKS, CT, HEADS, HD)
    coarse_values = jnp.dot(coarse_flat, coarse_value, preferred_element_type=jnp.float32).astype(jnp.bfloat16).reshape(CBLOCKS, CT, HEADS, HD)
    row_flags = jnp.arange(row_total, dtype=jnp.int32) + shift_row >= row_total
    column_flag = jnp.arange(column_count, dtype=jnp.int32) + shift_col >= column_count

    def one_strip(strip_index):
        start_row = (strip_index * SR).astype(jnp.int32)
        picked = block_table[strip_index]
        strip_keys = coarse_keys[picked].reshape(NB * CT, HEADS, HD)
        strip_values = coarse_values[picked].reshape(NB * CT, HEADS, HD)
        return attend(lax.dynamic_slice_in_dim(queries, start_row, SR, 0), lax.dynamic_slice_in_dim(keys_fine, start_row, SR, 0), lax.dynamic_slice_in_dim(values_fine, start_row, SR, 0), strip_keys, strip_values, lax.dynamic_slice_in_dim(row_flags, start_row, SR, 0), column_flag)
    head_out = lax.map(one_strip, jnp.arange(STRIPS, dtype=jnp.int32)).reshape(-1, FD)
    attn_sum = jnp.dot(head_out, w_out, preferred_element_type=jnp.float32)
    mid = flat_rows.astype(jnp.float32) + attn_sum
    normed_mid = rms_scale(mid, mlp_gain).astype(jnp.bfloat16)
    gate_term = jnp.dot(normed_mid, w_gate, preferred_element_type=jnp.float32)
    up_term = jnp.dot(normed_mid, w_up, preferred_element_type=jnp.float32)
    hidden = (jax.nn.silu(gate_term) * up_term).astype(jnp.bfloat16)
    mlp_sum = jnp.dot(hidden, w_down, preferred_element_type=jnp.float32)
    block_out = (mid + mlp_sum).astype(jnp.bfloat16).reshape(row_total, column_count, FD)
    return jnp.roll(block_out, (shift_row, shift_col), axis=(0, 1))
```

```python
import jax
import jax.numpy as jnp
from jax import lax
from jax.experimental import pallas as pl
from jax.experimental.pallas import tpu as pltpu
from jax.sharding import PartitionSpec as P

HEADS = 8
HD = 64
WS = 8
EPS = 1e-06
F32 = jnp.float32
BF16 = jnp.bfloat16
LOW = -1e30
VMEM_LIMIT = 40 * 1024 * 1024


def iota(shape, dim):
    return lax.broadcasted_iota(jnp.int32, shape, dim)


def rms(x, gain):
    mean_square = jnp.mean(x * x, axis=-1, keepdims=True)
    return x * lax.rsqrt(mean_square + EPS) * gain


def local_blocks(ids, table, per_strip, total):
    first = (ids[0] - 1) * per_strip
    return [lax.rem(table[i] - first + 2 * total, total) for i in range(table.shape[0])]


def project_kernel(total, ids, table, coarse, w_k, w_v, fine, gain, w_q, kv, pay_o, pay_e, q_nat, q_t):
    step = pl.program_id(0)
    rows = coarse.shape[0]
    odd_head = lax.rem(ids[1], 2) == 1
    low = iota((rows, 128), 1) < HD
    tokens = coarse[...]
    key = jnp.dot(tokens, w_k[...], preferred_element_type=F32)
    value = jnp.dot(tokens, w_v[...], preferred_element_type=F32)
    key = jnp.where(odd_head, pltpu.roll(key, HD, 1), key)
    value = jnp.where(odd_head, value, pltpu.roll(value, HD, 1))
    both = jnp.where(low, key, value).astype(BF16)
    at = pl.ds(pl.multiple_of(step * rows, rows), rows)
    kv[at, :] = both
    pay_o[at, :] = both
    pay_e[at, :] = both

    @pl.when(step == 0)
    def _():
        x = fine[...]
        n_tok, width = x.shape
        base = kv.shape[0]
        half = n_tok // 2
        even = lax.rem(ids[0], 2) == 0
        top, bottom = x[:half], x[half:]
        for c in range(width // 128):
            lanes = slice(128 * c, 128 * c + 128)
            at_c = slice(base + half * c, base + half * (c + 1))
            t_c, b_c = top[:, lanes], bottom[:, lanes]
            pay_o[at_c, :] = jnp.where(even, t_c, b_c)
            pay_e[at_c, :] = jnp.where(even, b_c, t_c)
        chosen = local_blocks(ids, table, base // 128, total)
        lane = iota((16, 128), 1)
        marks = jnp.zeros((16, 128), F32)
        for i, b in enumerate(chosen):
            marks = jnp.where(lane == i, b.astype(F32), marks)
        end = base + half * (width // 128)
        pay_o[end : end + 16, :] = marks.astype(BF16)
        pay_e[end : end + 16, :] = marks.astype(BF16)
        normed = rms(x.astype(F32), gain[...]).astype(BF16)
        q = jnp.dot(normed, w_q[...], preferred_element_type=F32) * (1.0 / HD**0.5)
        q_nat[...] = q.astype(BF16)
        q_t[...] = q.T.astype(BF16).reshape(q_t.shape)


def project(ids, table, coarse, w_k, w_v, fine, gain, w_q, total):
    n_coarse, cw = coarse.shape
    n_tok, width = fine.shape
    steps = n_coarse // 128
    pay_rows = n_coarse + (n_tok // 2) * (width // 128) + 16
    whole = lambda *shape: pl.BlockSpec(shape, lambda i, *_: (0,) * len(shape))
    head_cols = pl.BlockSpec((cw, 128), lambda i, ids, table: (0, ids[1] // 2))
    return pl.pallas_call(
        lambda *refs: project_kernel(total, *refs),
        grid_spec=pltpu.PrefetchScalarGridSpec(
            num_scalar_prefetch=2,
            grid=(steps,),
            in_specs=[
                pl.BlockSpec((128, cw), lambda i, *_: (i, 0)),
                head_cols,
                head_cols,
                whole(n_tok, width),
                whole(1, width),
                whole(width, width),
            ],
            out_specs=[
                whole(n_coarse, 128),
                whole(pay_rows, 128),
                whole(pay_rows, 128),
                whole(n_tok, width),
                whole(HEADS, HD, n_tok),
            ],
        ),
        out_shape=[
            jax.ShapeDtypeStruct((n_coarse, 128), BF16),
            jax.ShapeDtypeStruct((pay_rows, 128), BF16),
            jax.ShapeDtypeStruct((pay_rows, 128), BF16),
            jax.ShapeDtypeStruct((n_tok, width), BF16),
            jax.ShapeDtypeStruct((HEADS, HD, n_tok), BF16),
        ],
        compiler_params=pltpu.CompilerParams(vmem_limit_bytes=VMEM_LIMIT),
        cost_estimate=pl.CostEstimate(flops=350_000_000, bytes_accessed=4_000_000, transcendentals=0),
        name="project",
    )(ids, table, coarse, w_k, w_v, fine, gain, w_q)


def stack_kernel(ids, base, got_o, got_e, fine, out):
    n_tok, width = fine.shape
    half = n_tok // 2
    out[half : half + n_tok, :] = fine[...]
    even = lax.rem(ids[0], 2) == 0
    for c in range(width // 128):
        lanes = slice(128 * c, 128 * c + 128)
        at = slice(base + half * c, base + half * (c + 1))
        a, b = got_o[at, :], got_e[at, :]
        out[0:half, lanes] = jnp.where(even, a, b)
        out[half + n_tok :, lanes] = jnp.where(even, b, a)


def stack_rows(ids, got_o, got_e, fine, base):
    n_tok, width = fine.shape
    vmem = pl.BlockSpec(memory_space=pltpu.VMEM)
    return pl.pallas_call(
        lambda ids, a, b, x, out: stack_kernel(ids, base, a, b, x, out),
        in_specs=[pl.BlockSpec(memory_space=pltpu.SMEM), vmem, vmem, vmem],
        out_specs=vmem,
        out_shape=jax.ShapeDtypeStruct((2 * n_tok, width), BF16),
        compiler_params=pltpu.CompilerParams(vmem_limit_bytes=VMEM_LIMIT),
        cost_estimate=pl.CostEstimate(flops=0, bytes_accessed=1_000_000, transcendentals=0),
        name="stack_rows",
    )(ids, got_o, got_e, fine)


def window_kernel(last, ids, shifts, left, mid, right, q, gain, w_k, w_v, out, lse):
    span = left.shape[0]
    side = span - 64
    strip, member = ids[0], ids[1]
    shift_row, shift_col = shifts[0], shifts[1]
    fine = jnp.concatenate([left[...], mid[...], right[...]], axis=0).astype(F32)
    normed = rms(fine, gain[...]).astype(BF16)
    keys = jnp.dot(normed, w_k[...], preferred_element_type=F32).astype(BF16)
    values = jnp.dot(normed, w_v[...], preferred_element_type=F32).astype(BF16)
    shape = (128, 3 * side)
    query = lax.rem(iota(shape, 0), 64)
    column_q = lax.rem(query, 8)
    key = iota(shape, 1)
    part = (key >= side).astype(jnp.int32) + (key >= 2 * side).astype(jnp.int32)
    within = key - part * side
    column_k = (part - 1) * 8 + lax.rem(within, 8)
    same_col = lax.shift_right_arithmetic(column_q - shift_col + 16, 3) == lax.shift_right_arithmetic(
        column_k - shift_col + 16, 3
    )
    wrap_col = ((column_k < 0) & (member == 0)) | ((column_k > 7) & (member == last[1]))
    lane = iota((64, 128), 1)
    low = lane < HD
    low_rows = iota((128, 128), 0) < 64
    low_lanes = iota((128, 128), 1) < HD
    own = low_rows == low_lanes
    for half in range(2):
        row_q = 8 * half + lax.shift_right_arithmetic(query, 3)
        row_k = 8 * half - 8 + lax.shift_right_arithmetic(within, 3)
        same_row = lax.shift_right_arithmetic(row_q - shift_row + 16, 3) == lax.shift_right_arithmetic(
            row_k - shift_row + 16, 3
        )
        wrap_row = ((row_k < 0) & (strip == 0)) | ((row_k > 15) & (strip == last[0]))
        seen = same_row & same_col & jnp.logical_not(wrap_row | wrap_col)
        rows = slice(64 * half, 64 * half + 64)
        pick = lambda a: jnp.concatenate(
            [a[span * b + 64 * half : span * b + 64 * half + side] for b in range(3)], axis=0
        )
        keys_h, values_h = pick(keys), pick(values)
        marks = jnp.zeros((64, 128), F32)
        for pair in range(HEADS // 2):
            lanes = slice(128 * pair, 128 * pair + 128)
            q_pair = q[rows, lanes]
            q_both = jnp.concatenate([q_pair, q_pair], axis=0)
            q_both = jnp.where(own, q_both, jnp.zeros_like(q_both))
            score = lax.dot_general(
                q_both, keys_h[:, lanes], (((1,), (1,)), ((), ())), preferred_element_type=F32
            )
            score = jnp.where(seen, score, LOW)
            peak = jnp.max(score, axis=-1, keepdims=True)
            weight = jnp.exp(score - peak)
            total = jnp.sum(weight, axis=-1, keepdims=True)
            mixed = jnp.dot(weight.astype(BF16), values_h[:, lanes], preferred_element_type=F32) / total
            out[rows, lanes] = jnp.where(low, mixed[:64], mixed[64:])
            level = peak + jnp.log(total)
            marks = jnp.where(lane == 2 * pair, level[:64], marks)
            marks = jnp.where(lane == 2 * pair + 1, level[64:], marks)
        lse[rows, :] = marks


def window_attention(ids, shifts, left, mid, right, q, gain, w_k, w_v, last):
    n_tok, width = q.shape
    vmem = pl.BlockSpec(memory_space=pltpu.VMEM)
    smem = pl.BlockSpec(memory_space=pltpu.SMEM)
    return pl.pallas_call(
        lambda *refs: window_kernel(last, *refs),
        in_specs=[smem, smem] + [vmem] * 7,
        out_specs=[vmem, vmem],
        out_shape=[
            jax.ShapeDtypeStruct((n_tok, width), F32),
            jax.ShapeDtypeStruct((n_tok, 128), F32),
        ],
        compiler_params=pltpu.CompilerParams(vmem_limit_bytes=VMEM_LIMIT),
        cost_estimate=pl.CostEstimate(flops=2_000_000_000, bytes_accessed=3_000_000, transcendentals=600_000),
        name="window_attention",
    )(ids, shifts, left, mid, right, q, gain, w_k, w_v)


def coarse_kernel(total, ids, shifts, table, table_before, q_t, own, got_o, got_e, far_even, far_odd, out, store):
    n_own = own.shape[0]
    per_strip = n_own // 128
    even = lax.rem(ids[0], 2) == 0
    store[2 * per_strip : 3 * per_strip] = own[...].reshape(per_strip, 128, 128)

    @pl.when(even)
    def _():
        store[0:per_strip] = far_even[...].reshape(per_strip, 128, 128)
        store[per_strip : 2 * per_strip] = got_o[0:n_own, :].reshape(per_strip, 128, 128)
        store[3 * per_strip :] = got_e[0:n_own, :].reshape(per_strip, 128, 128)

    @pl.when(jnp.logical_not(even))
    def _():
        store[0:per_strip] = far_odd[0:n_own, :].reshape(per_strip, 128, 128)
        store[per_strip : 2 * per_strip] = got_e[0:n_own, :].reshape(per_strip, 128, 128)
        store[3 * per_strip :] = got_o[0:n_own, :].reshape(per_strip, 128, 128)

    here = [b + per_strip for b in local_blocks(ids, table, per_strip, total)]
    before = [table_before[i] for i in range(table_before.shape[0])]
    kv_here = jnp.concatenate([store[b] for b in here], axis=0)
    kv_before = jnp.concatenate([store[b] for b in before], axis=0)
    kv_here_t = kv_here.astype(F32).T.astype(BF16)
    kv_before_t = kv_before.astype(F32).T.astype(BF16)
    shift_row = shifts[0]
    lane = lax.rem(iota((1, 256), 1), 128)
    earlier = lane < WS * shift_row
    line = iota((16, 256), 0)
    members = q_t.shape[0]
    for p in range(members // 2):
        q = jnp.concatenate([q_t[2 * p], q_t[2 * p + 1]], axis=1)
        q = jnp.concatenate([q, jnp.zeros_like(q)], axis=0)
        score = jnp.where(
            earlier,
            jnp.dot(kv_before, q, preferred_element_type=F32),
            jnp.dot(kv_here, q, preferred_element_type=F32),
        )
        peak = jnp.max(score, axis=0, keepdims=True)
        weight = jnp.exp(score - peak)
        sums = jnp.sum(weight, axis=0, keepdims=True)
        weight = weight.astype(BF16)
        mixed = jnp.where(
            earlier,
            jnp.dot(kv_before_t, weight, preferred_element_type=F32),
            jnp.dot(kv_here_t, weight, preferred_element_type=F32),
        )
        mixed = (mixed[HD:] / sums).astype(BF16)
        level = peak + jnp.log(sums)
        first = level.astype(BF16).astype(F32)
        second = (level - first).astype(BF16).astype(F32)
        third = level - first - second
        marks = jnp.where(line == 0, first, jnp.where(line == 1, second, jnp.where(line == 2, third, 0.0)))
        marks = marks.astype(BF16)
        for k in range(2):
            lanes = slice(128 * k, 128 * k + 128)
            out[2 * p + k, 0:HD, :] = mixed[:, lanes]
            out[2 * p + k, HD : HD + 16, :] = marks[:, lanes]


def coarse_attention(ids, shifts, table, table_before, q_t, own, got_o, got_e, far_even, far_odd, total):
    vmem = pl.BlockSpec(memory_space=pltpu.VMEM)
    smem = pl.BlockSpec(memory_space=pltpu.SMEM)
    members, _, n_tok = q_t.shape
    return pl.pallas_call(
        lambda *refs: coarse_kernel(total, *refs),
        in_specs=[smem] * 4 + [vmem] * 6,
        out_specs=vmem,
        out_shape=jax.ShapeDtypeStruct((members, HD + 16, n_tok), BF16),
        scratch_shapes=[pltpu.VMEM((4 * own.shape[0] // 128, 128, 128), BF16)],
        compiler_params=pltpu.CompilerParams(vmem_limit_bytes=VMEM_LIMIT),
        cost_estimate=pl.CostEstimate(flops=1_600_000_000, bytes_accessed=1_500_000, transcendentals=1_000_000),
        name="coarse_attention",
    )(ids, shifts, table, table_before, q_t, own, got_o, got_e, far_even, far_odd)


def finish_kernel(fine, near, near_lse, coarse, w_out, gain, w_gate, w_up, w_down, out, mid, normed, acc):
    step = pl.program_id(0)

    @pl.when(step == 0)
    def _():
        heads = coarse.shape[0]
        far = jnp.concatenate([coarse[h, 0:HD, :].astype(F32) for h in range(heads)], axis=0).T
        marks = [coarse[h, HD : HD + 16, :].astype(F32) for h in range(heads)]
        level = jnp.concatenate([m[0:1] + m[1:2] + m[2:3] for m in marks], axis=0).T
        diff = near_lse[:, 0:heads] - level
        share = 1.0 / (1.0 + jnp.exp(diff))
        share = jnp.concatenate(
            [jnp.broadcast_to(share[:, h : h + 1], (share.shape[0], HD)) for h in range(heads)], axis=1
        )
        head_out = (near[...] * (1.0 - share) + far * share).astype(BF16)
        m = fine[...].astype(F32) + jnp.dot(head_out, w_out[...], preferred_element_type=F32)
        mid[...] = m
        normed[...] = rms(m, gain[...]).astype(BF16)
        acc[...] = jnp.zeros_like(acc)

    gate = jnp.dot(normed[...], w_gate[...], preferred_element_type=F32)
    up = jnp.dot(normed[...], w_up[...], preferred_element_type=F32)
    hidden = (gate * (1.0 / (1.0 + jnp.exp(-gate))) * up).astype(BF16)
    acc[...] += jnp.dot(hidden, w_down[...], preferred_element_type=F32)

    @pl.when(step == pl.num_programs(0) - 1)
    def _():
        out[...] = (mid[...] + acc[...]).astype(BF16)


def finish(fine, near, near_lse, coarse, w_out, gain, w_gate, w_up, w_down):
    n_tok, width = fine.shape
    ff = w_gate.shape[1]
    chunk = 512
    whole = lambda *shape: pl.BlockSpec(shape, lambda i: (0,) * len(shape))
    return pl.pallas_call(
        finish_kernel,
        grid=(ff // chunk,),
        in_specs=[
            whole(n_tok, width),
            whole(n_tok, width),
            whole(*near_lse.shape),
            whole(*coarse.shape),
            whole(width, width),
            whole(1, width),
            pl.BlockSpec((width, chunk), lambda i: (0, i)),
            pl.BlockSpec((width, chunk), lambda i: (0, i)),
            pl.BlockSpec((chunk, width), lambda i: (i, 0)),
        ],
        out_specs=whole(n_tok, width),
        out_shape=jax.ShapeDtypeStruct((n_tok, width), BF16),
        scratch_shapes=[
            pltpu.VMEM((n_tok, width), F32),
            pltpu.VMEM((n_tok, width), BF16),
            pltpu.VMEM((n_tok, width), F32),
        ],
        compiler_params=pltpu.CompilerParams(vmem_limit_bytes=VMEM_LIMIT),
        cost_estimate=pl.CostEstimate(flops=900_000_000, bytes_accessed=7_500_000, transcendentals=300_000),
        name="finish",
    )(fine, near, near_lse, coarse, w_out, gain, w_gate, w_up, w_down)


def local(
    fine,
    coarse,
    block_table,
    shifts,
    attn_gain,
    w_query,
    w_key,
    w_value,
    w_out,
    coarse_key,
    coarse_value,
    mlp_gain,
    w_gate,
    w_up,
    w_down,
):
    strips = lax.axis_size("tile")
    members = lax.axis_size("narrow")
    strip = lax.axis_index("tile").astype(jnp.int32)
    member = lax.axis_index("narrow").astype(jnp.int32)
    ids = jnp.stack([strip, member])
    rows, columns, width = fine.shape
    blocks, block_tokens, cw = coarse.shape
    total = blocks * strips
    n_own = blocks * block_tokens
    flat = fine.reshape(rows * columns, width)
    table = block_table.reshape(-1)
    gain = attn_gain.reshape(1, width)

    kv, pay_o, pay_e, q, q_t = project(
        ids, table, coarse.reshape(n_own, cw), coarse_key, coarse_value, flat, gain, w_query, total
    )
    odd_pairs = [(i, (i - 1) % strips if i % 2 == 0 else (i + 1) % strips) for i in range(strips)]
    even_pairs = [(i, i ^ 1) for i in range(strips)]
    got_o = lax.ppermute(pay_o, "tile", odd_pairs)
    got_e = lax.ppermute(pay_e, "tile", even_pairs)
    far_even = lax.ppermute(kv, "tile", [(i, (i + 2) % strips) for i in range(0, strips, 2)])
    q_head = lax.all_to_all(q_t, "narrow", 0, 0, tiled=True)
    far_odd = lax.ppermute(got_o, "tile", [(i, i + 1) for i in range(0, strips, 2)])

    stacked = stack_rows(ids, got_o, got_e, flat, n_own)
    right_of = lax.ppermute(stacked, "narrow", [(i, (i - 1) % members) for i in range(members)])
    left_of = lax.ppermute(stacked, "narrow", [(i, (i + 1) % members) for i in range(members)])
    mark_row = n_own + rows * columns // 2 * (width // 128)
    table_before = jnp.where(strip % 2 == 0, got_o[mark_row, :8], got_e[mark_row, :8]).astype(jnp.int32)

    far = coarse_attention(
        ids, shifts, table, table_before, q_head, kv, got_o, got_e, far_even, far_odd, total
    )
    far = lax.all_to_all(far, "narrow", 0, 0, tiled=True)
    near, near_lse = window_attention(
        ids, shifts, left_of, stacked, right_of, q, gain, w_key, w_value, (strips - 1, members - 1)
    )
    out = finish(
        flat, near, near_lse, far, w_out, mlp_gain.reshape(1, width), w_gate, w_up, w_down
    )
    return out.reshape(rows, columns, width)


def solution(mesh):
    placed = (
        P("tile", "narrow", None),
        P("tile", None, None),
        P("tile", None),
    ) + (P(),) * 12
    return jax.shard_map(
        local, mesh=mesh, in_specs=placed, out_specs=P("tile", "narrow", None), check_vma=False
    )
```

```python
import jax
import jax.numpy as jnp
from jax import lax
from jax.experimental import pallas as pl
from jax.experimental.pallas import tpu as pltpu
from jax.sharding import PartitionSpec as P

HEADS = 8
HD = 64
WS = 8
EPS = 1e-06
F32 = jnp.float32
BF16 = jnp.bfloat16
LOW = -1e30
VMEM_LIMIT = 24 * 1024 * 1024
COST = pl.CostEstimate(flops=1000, bytes_accessed=1000, transcendentals=0)


def iota(shape, dim):
    return lax.broadcasted_iota(jnp.int32, shape, dim)


def rms(x, gain):
    mean_square = jnp.mean(x * x, axis=-1, keepdims=True)
    return x * lax.rsqrt(mean_square + EPS) * gain


def local_blocks(ids, table, per_strip, total):
    first = (ids[0] - 1) * per_strip
    return [lax.rem(table[i] - first + 2 * total, total) for i in range(table.shape[0])]


def project_kernel(total, ids, table, coarse, w_k, w_v, fine, kv, pay_o, pay_e, c_buf, k_buf, v_buf, x_buf, sems):
    chunks = c_buf.shape[0]
    rows = c_buf.shape[1]
    cols = pl.ds(pl.multiple_of(ids[1] // 2 * 128, 128), 128)
    loads = [
        pltpu.make_async_copy(w_k.at[:, cols], k_buf, sems.at[0]),
        pltpu.make_async_copy(w_v.at[:, cols], v_buf, sems.at[1]),
        pltpu.make_async_copy(fine, x_buf, sems.at[2]),
    ]
    parts = [
        pltpu.make_async_copy(coarse.at[pl.ds(rows * i, rows)], c_buf.at[i], sems.at[3 + i])
        for i in range(chunks)
    ]
    for copy in (loads[0], loads[1], parts[0], loads[2], *parts[1:]):
        copy.start()
    odd_head = lax.rem(ids[1], 2) == 1
    even = lax.rem(ids[0], 2) == 0
    low = iota((rows, 128), 1) < HD
    base = kv.shape[0]
    n_tok, width = x_buf.shape
    half = n_tok // 2
    chosen = local_blocks(ids, table, base // 128, total)
    lane = iota((16, 128), 1)
    marks = jnp.zeros((16, 128), F32)
    for i, b in enumerate(chosen):
        marks = jnp.where(lane == i, b.astype(F32), marks)
    end = base + half * (width // 128)
    pay_o[end : end + 16, :] = marks.astype(BF16)
    pay_e[end : end + 16, :] = marks.astype(BF16)
    loads[0].wait()
    loads[1].wait()
    for i in range(chunks):
        parts[i].wait()
        tokens = c_buf[i]
        key = jnp.dot(tokens, k_buf[...], preferred_element_type=F32)
        value = jnp.dot(tokens, v_buf[...], preferred_element_type=F32)
        key = jnp.where(odd_head, pltpu.roll(key, HD, 1), key)
        value = jnp.where(odd_head, value, pltpu.roll(value, HD, 1))
        both = jnp.where(low, key, value).astype(BF16)
        at = slice(rows * i, rows * i + rows)
        kv[at, :] = both
        pay_o[at, :] = both
        pay_e[at, :] = both
    loads[2].wait()
    for c in range(width // 128):
        lanes = slice(128 * c, 128 * c + 128)
        at = slice(base + half * c, base + half * (c + 1))
        top, bottom = x_buf[0:half, lanes], x_buf[half:, lanes]
        pay_o[at, :] = jnp.where(even, top, bottom)
        pay_e[at, :] = jnp.where(even, bottom, top)


def project(ids, table, coarse, w_k, w_v, fine, total):
    n_coarse, cw = coarse.shape
    n_tok, width = fine.shape
    chunks = 4
    pay_rows = n_coarse + (n_tok // 2) * (width // 128) + 16
    smem = pl.BlockSpec(memory_space=pltpu.SMEM)
    hbm = pl.BlockSpec(memory_space=pltpu.HBM)
    vmem = pl.BlockSpec(memory_space=pltpu.VMEM)
    return pl.pallas_call(
        lambda *refs: project_kernel(total, *refs),
        in_specs=[smem, smem] + [hbm] * 4,
        out_specs=[vmem] * 3,
        out_shape=[
            jax.ShapeDtypeStruct((n_coarse, 128), BF16),
            jax.ShapeDtypeStruct((pay_rows, 128), BF16),
            jax.ShapeDtypeStruct((pay_rows, 128), BF16),
        ],
        scratch_shapes=[
            pltpu.VMEM((chunks, n_coarse // chunks, cw), BF16),
            pltpu.VMEM((cw, 128), BF16),
            pltpu.VMEM((cw, 128), BF16),
            pltpu.VMEM((n_tok, width), BF16),
            pltpu.SemaphoreType.DMA((3 + chunks,)),
        ],
        compiler_params=pltpu.CompilerParams(vmem_limit_bytes=VMEM_LIMIT),
        cost_estimate=COST,
        name="project",
    )(ids, table, coarse, w_k, w_v, fine)


def query_kernel(after, fine, gain, w_q, q_nat, q_t, x_buf, q_buf, sems):
    first = pltpu.make_async_copy(fine, x_buf, sems.at[0])
    second = pltpu.make_async_copy(w_q, q_buf, sems.at[1])
    first.start()
    second.start()
    first.wait()
    normed = rms(x_buf[...].astype(F32), gain[...]).astype(BF16)
    second.wait()
    q = jnp.dot(normed, q_buf[...], preferred_element_type=F32) * (1.0 / HD**0.5)
    q_nat[...] = q.astype(BF16)
    q_t[...] = q.T.astype(BF16).reshape(q_t.shape)


def queries(after, fine, gain, w_q):
    n_tok, width = fine.shape
    hbm = pl.BlockSpec(memory_space=pltpu.HBM)
    vmem = pl.BlockSpec(memory_space=pltpu.VMEM)
    return pl.pallas_call(
        query_kernel,
        in_specs=[pl.BlockSpec(memory_space=pl.ANY), hbm, vmem, hbm],
        out_specs=[vmem] * 2,
        out_shape=[
            jax.ShapeDtypeStruct((n_tok, width), BF16),
            jax.ShapeDtypeStruct((HEADS, HD, n_tok), BF16),
        ],
        scratch_shapes=[
            pltpu.VMEM((n_tok, width), BF16),
            pltpu.VMEM((width, width), BF16),
            pltpu.SemaphoreType.DMA((2,)),
        ],
        compiler_params=pltpu.CompilerParams(vmem_limit_bytes=VMEM_LIMIT),
        cost_estimate=COST,
        name="queries",
    )(after, fine, gain, w_q)


def stack_kernel(ids, base, got_o, got_e, fine, out):
    n_tok, width = fine.shape
    half = n_tok // 2
    out[half : half + n_tok, :] = fine[...]
    even = lax.rem(ids[0], 2) == 0
    for c in range(width // 128):
        lanes = slice(128 * c, 128 * c + 128)
        at = slice(base + half * c, base + half * (c + 1))
        a, b = got_o[at, :], got_e[at, :]
        out[0:half, lanes] = jnp.where(even, a, b)
        out[half + n_tok :, lanes] = jnp.where(even, b, a)


def stack_rows(ids, got_o, got_e, fine, base):
    n_tok, width = fine.shape
    vmem = pl.BlockSpec(memory_space=pltpu.VMEM)
    return pl.pallas_call(
        lambda ids, a, b, x, out: stack_kernel(ids, base, a, b, x, out),
        in_specs=[pl.BlockSpec(memory_space=pltpu.SMEM), vmem, vmem, vmem],
        out_specs=vmem,
        out_shape=jax.ShapeDtypeStruct((2 * n_tok, width), BF16),
        compiler_params=pltpu.CompilerParams(vmem_limit_bytes=VMEM_LIMIT),
        cost_estimate=pl.CostEstimate(flops=10000000000, bytes_accessed=33333333, transcendentals=0),
        name="stack_rows",
    )(ids, got_o, got_e, fine)


def window_kernel(last, ids, shifts, left, mid, right, q, gain, w_k, w_v, out, lse, k_buf, v_buf, sems):
    loads = [pltpu.make_async_copy(w_k, k_buf, sems.at[0]), pltpu.make_async_copy(w_v, v_buf, sems.at[1])]
    for copy in loads:
        copy.start()
    span = left.shape[0]
    side = span - 64
    strip, member = ids[0], ids[1]
    shift_row, shift_col = shifts[0], shifts[1]
    fine = jnp.concatenate([left[...], mid[...], right[...]], axis=0).astype(F32)
    normed = rms(fine, gain[...]).astype(BF16)
    loads[0].wait()
    keys = jnp.dot(normed, k_buf[...], preferred_element_type=F32).astype(BF16)
    loads[1].wait()
    values = jnp.dot(normed, v_buf[...], preferred_element_type=F32).astype(BF16)
    shape = (128, 3 * side)
    query = lax.rem(iota(shape, 0), 64)
    column_q = lax.rem(query, 8)
    key = iota(shape, 1)
    part = (key >= side).astype(jnp.int32) + (key >= 2 * side).astype(jnp.int32)
    within = key - part * side
    column_k = (part - 1) * 8 + lax.rem(within, 8)
    same_col = lax.shift_right_arithmetic(column_q - shift_col + 16, 3) == lax.shift_right_arithmetic(
        column_k - shift_col + 16, 3
    )
    wrap_col = ((column_k < 0) & (member == 0)) | ((column_k > 7) & (member == last[1]))
    lane = iota((64, 128), 1)
    low = lane < HD
    low_rows = iota((128, 128), 0) < 64
    low_lanes = iota((128, 128), 1) < HD
    own = low_rows == low_lanes
    for half in range(2):
        row_q = 8 * half + lax.shift_right_arithmetic(query, 3)
        row_k = 8 * half - 8 + lax.shift_right_arithmetic(within, 3)
        same_row = lax.shift_right_arithmetic(row_q - shift_row + 16, 3) == lax.shift_right_arithmetic(
            row_k - shift_row + 16, 3
        )
        wrap_row = ((row_k < 0) & (strip == 0)) | ((row_k > 15) & (strip == last[0]))
        seen = same_row & same_col & jnp.logical_not(wrap_row | wrap_col)
        rows = slice(64 * half, 64 * half + 64)
        pick = lambda a: jnp.concatenate(
            [a[span * b + 64 * half : span * b + 64 * half + side] for b in range(3)], axis=0
        )
        keys_h, values_h = pick(keys), pick(values)
        marks = jnp.zeros((64, 128), F32)
        for pair in range(HEADS // 2):
            lanes = slice(128 * pair, 128 * pair + 128)
            q_pair = q[rows, lanes]
            q_both = jnp.concatenate([q_pair, q_pair], axis=0)
            q_both = jnp.where(own, q_both, jnp.zeros_like(q_both))
            score = lax.dot_general(
                q_both, keys_h[:, lanes], (((1,), (1,)), ((), ())), preferred_element_type=F32
            )
            score = jnp.where(seen, score, LOW)
            peak = jnp.max(score, axis=-1, keepdims=True)
            weight = jnp.exp(score - peak)
            total = jnp.sum(weight, axis=-1, keepdims=True)
            mixed = jnp.dot(weight.astype(BF16), values_h[:, lanes], preferred_element_type=F32) / total
            out[rows, lanes] = jnp.where(low, mixed[:64], mixed[64:])
            level = peak + jnp.log(total)
            marks = jnp.where(lane == 2 * pair, level[:64], marks)
            marks = jnp.where(lane == 2 * pair + 1, level[64:], marks)
        lse[rows, :] = marks


def window_attention(ids, shifts, left, mid, right, q, gain, w_k, w_v, last):
    n_tok, width = q.shape
    vmem = pl.BlockSpec(memory_space=pltpu.VMEM)
    smem = pl.BlockSpec(memory_space=pltpu.SMEM)
    return pl.pallas_call(
        lambda *refs: window_kernel(last, *refs),
        in_specs=[smem, smem] + [vmem] * 5 + [pl.BlockSpec(memory_space=pltpu.HBM)] * 2,
        out_specs=[vmem, vmem],
        out_shape=[
            jax.ShapeDtypeStruct((n_tok, width), F32),
            jax.ShapeDtypeStruct((n_tok, 128), F32),
        ],
        scratch_shapes=[
            pltpu.VMEM((width, width), BF16),
            pltpu.VMEM((width, width), BF16),
            pltpu.SemaphoreType.DMA((2,)),
        ],
        compiler_params=pltpu.CompilerParams(vmem_limit_bytes=VMEM_LIMIT),
        cost_estimate=COST,
        name="window_attention",
    )(ids, shifts, left, mid, right, q, gain, w_k, w_v)


def coarse_kernel(total, after, after_too, ids, shifts, table, table_before, q_t, own, got_o, got_e, far_even, far_odd, out, store):
    n_own = own.shape[0]
    per_strip = n_own // 128
    even = lax.rem(ids[0], 2) == 0
    store[2 * per_strip : 3 * per_strip] = own[...].reshape(per_strip, 128, 128)

    @pl.when(even)
    def _():
        store[0:per_strip] = far_even[...].reshape(per_strip, 128, 128)
        store[per_strip : 2 * per_strip] = got_o[0:n_own, :].reshape(per_strip, 128, 128)
        store[3 * per_strip :] = got_e[0:n_own, :].reshape(per_strip, 128, 128)

    @pl.when(jnp.logical_not(even))
    def _():
        store[0:per_strip] = far_odd[0:n_own, :].reshape(per_strip, 128, 128)
        store[per_strip : 2 * per_strip] = got_e[0:n_own, :].reshape(per_strip, 128, 128)
        store[3 * per_strip :] = got_o[0:n_own, :].reshape(per_strip, 128, 128)

    here = [b + per_strip for b in local_blocks(ids, table, per_strip, total)]
    before = [table_before[i] for i in range(table_before.shape[0])]
    kv_here = jnp.concatenate([store[b] for b in here], axis=0)
    kv_before = jnp.concatenate([store[b] for b in before], axis=0)
    kv_here_t = kv_here.astype(F32).T.astype(BF16)
    kv_before_t = kv_before.astype(F32).T.astype(BF16)
    shift_row = shifts[0]
    lane = lax.rem(iota((1, 256), 1), 128)
    earlier = lane < WS * shift_row
    line = iota((16, 256), 0)
    members = q_t.shape[0]
    for p in range(members // 2):
        q = jnp.concatenate([q_t[2 * p], q_t[2 * p + 1]], axis=1)
        q = jnp.concatenate([q, jnp.zeros_like(q)], axis=0)
        score = jnp.where(
            earlier,
            jnp.dot(kv_before, q, preferred_element_type=F32),
            jnp.dot(kv_here, q, preferred_element_type=F32),
        )
        peak = jnp.max(score, axis=0, keepdims=True)
        weight = jnp.exp(score - peak)
        sums = jnp.sum(weight, axis=0, keepdims=True)
        weight = weight.astype(BF16)
        mixed = jnp.where(
            earlier,
            jnp.dot(kv_before_t, weight, preferred_element_type=F32),
            jnp.dot(kv_here_t, weight, preferred_element_type=F32),
        )
        mixed = (mixed[HD:] / sums).astype(BF16)
        level = peak + jnp.log(sums)
        first = level.astype(BF16).astype(F32)
        second = (level - first).astype(BF16).astype(F32)
        third = level - first - second
        marks = jnp.where(line == 0, first, jnp.where(line == 1, second, jnp.where(line == 2, third, 0.0)))
        marks = marks.astype(BF16)
        for k in range(2):
            lanes = slice(128 * k, 128 * k + 128)
            out[2 * p + k, 0:HD, :] = mixed[:, lanes]
            out[2 * p + k, HD : HD + 16, :] = marks[:, lanes]


def coarse_attention(after, after_too, ids, shifts, table, table_before, q_t, own, got_o, got_e, far_even, far_odd, total):
    vmem = pl.BlockSpec(memory_space=pltpu.VMEM)
    smem = pl.BlockSpec(memory_space=pltpu.SMEM)
    members, _, n_tok = q_t.shape
    return pl.pallas_call(
        lambda *refs: coarse_kernel(total, *refs),
        in_specs=[pl.BlockSpec(memory_space=pl.ANY)] * 2 + [smem] * 4 + [vmem] * 6,
        out_specs=vmem,
        out_shape=jax.ShapeDtypeStruct((members, HD + 16, n_tok), BF16),
        scratch_shapes=[pltpu.VMEM((4 * own.shape[0] // 128, 128, 128), BF16)],
        compiler_params=pltpu.CompilerParams(vmem_limit_bytes=VMEM_LIMIT),
        cost_estimate=COST,
        name="coarse_attention",
    )(after, after_too, ids, shifts, table, table_before, q_t, own, got_o, got_e, far_even, far_odd)


def finish_kernel(
    fine, near, near_lse, coarse, gain, w_out, w_gate, w_up, w_down, out, o_buf, g_buf, u_buf, d_buf, sems
):
    steps, width, chunk = g_buf.shape
    first = pltpu.make_async_copy(w_out, o_buf, sems.at[0])
    first.start()
    loads = []
    for i in range(steps):
        at = pl.ds(chunk * i, chunk)
        loads.append(
            [
                pltpu.make_async_copy(w_gate.at[:, at], g_buf.at[i], sems.at[1 + 3 * i]),
                pltpu.make_async_copy(w_up.at[:, at], u_buf.at[i], sems.at[2 + 3 * i]),
                pltpu.make_async_copy(w_down.at[at], d_buf.at[i], sems.at[3 + 3 * i]),
            ]
        )
        for copy in loads[i]:
            copy.start()
    heads = coarse.shape[0]
    far = jnp.concatenate([coarse[h, 0:HD, :].astype(F32) for h in range(heads)], axis=0).T
    marks = [coarse[h, HD : HD + 16, :].astype(F32) for h in range(heads)]
    level = jnp.concatenate([m[0:1] + m[1:2] + m[2:3] for m in marks], axis=0).T
    diff = near_lse[:, 0:heads] - level
    share = 1.0 / (1.0 + jnp.exp(diff))
    share = jnp.concatenate(
        [jnp.broadcast_to(share[:, h : h + 1], (share.shape[0], HD)) for h in range(heads)], axis=1
    )
    head_out = (near[...] * (1.0 - share) + far * share).astype(BF16)
    first.wait()
    mid = fine[...].astype(F32) + jnp.dot(head_out, o_buf[...], preferred_element_type=F32)
    normed = rms(mid, gain[...]).astype(BF16)
    total = mid
    for i in range(steps):
        loads[i][0].wait()
        gate = jnp.dot(normed, g_buf[i], preferred_element_type=F32)
        loads[i][1].wait()
        up = jnp.dot(normed, u_buf[i], preferred_element_type=F32)
        hidden = (gate * (1.0 / (1.0 + jnp.exp(-gate))) * up).astype(BF16)
        loads[i][2].wait()
        total = total + jnp.dot(hidden, d_buf[i], preferred_element_type=F32)
    out[...] = total.astype(BF16)


def finish(fine, near, near_lse, coarse, gain, w_out, w_gate, w_up, w_down):
    n_tok, width = fine.shape
    ff = w_gate.shape[1]
    chunk = 512
    vmem = pl.BlockSpec(memory_space=pltpu.VMEM)
    hbm = pl.BlockSpec(memory_space=pltpu.HBM)
    return pl.pallas_call(
        finish_kernel,
        in_specs=[vmem] * 5 + [hbm] * 4,
        out_specs=vmem,
        out_shape=jax.ShapeDtypeStruct((n_tok, width), BF16),
        scratch_shapes=[
            pltpu.VMEM((width, width), BF16),
            pltpu.VMEM((ff // chunk, width, chunk), BF16),
            pltpu.VMEM((ff // chunk, width, chunk), BF16),
            pltpu.VMEM((ff // chunk, chunk, width), BF16),
            pltpu.SemaphoreType.DMA((1 + 3 * (ff // chunk),)),
        ],
        compiler_params=pltpu.CompilerParams(vmem_limit_bytes=VMEM_LIMIT),
        cost_estimate=COST,
        name="finish",
    )(fine, near, near_lse, coarse, gain, w_out, w_gate, w_up, w_down)


def local(
    fine,
    coarse,
    block_table,
    shifts,
    attn_gain,
    w_query,
    w_key,
    w_value,
    w_out,
    coarse_key,
    coarse_value,
    mlp_gain,
    w_gate,
    w_up,
    w_down,
):
    strips = lax.axis_size("tile")
    members = lax.axis_size("narrow")
    strip = lax.axis_index("tile").astype(jnp.int32)
    member = lax.axis_index("narrow").astype(jnp.int32)
    ids = jnp.stack([strip, member])
    rows, columns, width = fine.shape
    blocks, block_tokens, cw = coarse.shape
    total = blocks * strips
    n_own = blocks * block_tokens
    flat = fine.reshape(rows * columns, width)
    table = block_table.reshape(-1)
    gain = attn_gain.reshape(1, width)

    stay = lambda x: pltpu.with_memory_space_constraint(x, pltpu.HBM)
    flat_hbm = stay(flat)
    kv, pay_o, pay_e = project(
        ids, table, stay(coarse.reshape(n_own, cw)), stay(coarse_key), stay(coarse_value), flat_hbm, total
    )
    odd_pairs = [(i, (i - 1) % strips if i % 2 == 0 else (i + 1) % strips) for i in range(strips)]
    even_pairs = [(i, i ^ 1) for i in range(strips)]
    got_o = lax.ppermute(pay_o, "tile", odd_pairs)
    far_on = lax.ppermute(kv, "tile", [(i, (i + 3) % strips) for i in range(0, strips, 2)])
    got_e = lax.ppermute(pay_e, "tile", even_pairs)
    q, q_t = queries(got_e, flat_hbm, gain, stay(w_query))
    q_head = lax.all_to_all(q_t, "narrow", 0, 0, tiled=True)
    far_even = lax.ppermute(far_on, "tile", [(i + 1, i) for i in range(0, strips, 2)])
    far_odd = lax.ppermute(got_o, "tile", [(i, i + 1) for i in range(0, strips, 2)])

    stacked = stack_rows(ids, got_o, got_e, flat, n_own)
    stacked, q_head = lax.optimization_barrier((stacked, q_head))
    right_of = lax.ppermute(stacked, "narrow", [(i, (i - 1) % members) for i in range(members)])
    left_of = lax.ppermute(stacked, "narrow", [(i, (i + 1) % members) for i in range(members)])
    mark_row = n_own + rows * columns // 2 * (width // 128)
    table_before = jnp.where(strip % 2 == 0, got_o[mark_row, :8], got_e[mark_row, :8]).astype(jnp.int32)

    far = coarse_attention(
        left_of, right_of, ids, shifts, table, table_before, q_head, kv, got_o, got_e, far_even, far_odd, total
    )
    far = lax.all_to_all(far, "narrow", 0, 0, tiled=True)
    near, near_lse = window_attention(
        ids, shifts, left_of, stacked, right_of, q, gain, stay(w_key), stay(w_value), (strips - 1, members - 1)
    )
    out = finish(
        flat,
        near,
        near_lse,
        far,
        mlp_gain.reshape(1, width),
        stay(w_out),
        stay(w_gate),
        stay(w_up),
        stay(w_down),
    )
    return out.reshape(rows, columns, width)


def solution(mesh):
    placed = (
        P("tile", "narrow", None),
        P("tile", None, None),
        P("tile", None),
    ) + (P(),) * 12
    return jax.shard_map(
        local, mesh=mesh, in_specs=placed, out_specs=P("tile", "narrow", None), check_vma=False
    )
```

```python
import jax
import jax.numpy as jnp
from jax import lax
from jax.experimental import pallas as pl
from jax.experimental.pallas import tpu as pltpu
from jax.sharding import PartitionSpec as P

HEADS = 8
HD = 64
WS = 8
EPS = 1e-06
F32 = jnp.float32
BF16 = jnp.bfloat16
LOW = -1e30
VMEM_LIMIT = 24 * 1024 * 1024
COST = pl.CostEstimate(flops=1000, bytes_accessed=1000, transcendentals=0)
COST_ONWARD = pl.CostEstimate(flops=1000000000, bytes_accessed=1000, transcendentals=0)
COST_STACK = pl.CostEstimate(flops=10000000000, bytes_accessed=1000, transcendentals=0)
COST_CHOOSE = pl.CostEstimate(flops=10000000000, bytes_accessed=1000, transcendentals=0)
COST_COARSE = pl.CostEstimate(flops=1000, bytes_accessed=1000, transcendentals=0)


def iota(shape, dim):
    return lax.broadcasted_iota(jnp.int32, shape, dim)


def rms(x, gain):
    mean_square = jnp.mean(x * x, axis=-1, keepdims=True)
    return x * lax.rsqrt(mean_square + EPS) * gain


def local_blocks(ids, table, per_strip, total):
    first = (ids[0] - 1) * per_strip
    return [lax.rem(table[i] - first + 2 * total, total) for i in range(table.shape[0])]


def project_kernel(total, ids, table, coarse, w_k, w_v, fine, kv, pay_o, c_buf, w_buf, x_buf, sems):
    chunks = c_buf.shape[0]
    rows = c_buf.shape[1]
    cols = pl.ds(pl.multiple_of(ids[1] // 2 * 128, 128), 128)
    loads = [
        pltpu.make_async_copy(w_k.at[:, cols], w_buf.at[:, 0:128], sems.at[0]),
        pltpu.make_async_copy(w_v.at[:, cols], w_buf.at[:, 128:256], sems.at[1]),
        pltpu.make_async_copy(fine, x_buf, sems.at[2]),
    ]
    parts = [
        pltpu.make_async_copy(coarse.at[pl.ds(rows * i, rows)], c_buf.at[i], sems.at[3 + i])
        for i in range(chunks)
    ]
    for copy in (loads[0], loads[1], parts[0], loads[2], *parts[1:]):
        copy.start()
    odd_head = lax.rem(ids[1], 2) == 1
    even = lax.rem(ids[0], 2) == 0
    low = iota((rows, 128), 1) < HD
    base = kv.shape[0]
    n_tok, width = x_buf.shape
    half = n_tok // 2
    chosen = local_blocks(ids, table, base // 128, total)
    lane = iota((16, 128), 1)
    marks = jnp.zeros((16, 128), F32)
    for i, b in enumerate(chosen):
        marks = jnp.where(lane == i, b.astype(F32), marks)
    end = base + half * (width // 128)
    pay_o[end : end + 16, :] = marks.astype(BF16)
    loads[0].wait()
    loads[1].wait()
    for i in range(chunks):
        parts[i].wait()
        tokens = c_buf[i]
        product = jnp.dot(tokens, w_buf[...], preferred_element_type=F32)
        key, value = product[:, 0:128], product[:, 128:256]
        key = jnp.where(odd_head, pltpu.roll(key, HD, 1), key)
        value = jnp.where(odd_head, value, pltpu.roll(value, HD, 1))
        both = jnp.where(low, key, value).astype(BF16)
        at = slice(rows * i, rows * i + rows)
        kv[at, :] = both
        pay_o[at, :] = both
    loads[2].wait()
    for c in range(width // 128):
        lanes = slice(128 * c, 128 * c + 128)
        at = slice(base + half * c, base + half * (c + 1))
        top, bottom = x_buf[0:half, lanes], x_buf[half:, lanes]
        pay_o[at, :] = jnp.where(even, top, bottom)


def project(ids, table, coarse, w_k, w_v, fine, total):
    n_coarse, cw = coarse.shape
    n_tok, width = fine.shape
    chunks = 4
    pay_rows = n_coarse + (n_tok // 2) * (width // 128) + 16
    smem = pl.BlockSpec(memory_space=pltpu.SMEM)
    hbm = pl.BlockSpec(memory_space=pltpu.HBM)
    vmem = pl.BlockSpec(memory_space=pltpu.VMEM)
    return pl.pallas_call(
        lambda *refs: project_kernel(total, *refs),
        in_specs=[smem, smem] + [hbm] * 4,
        out_specs=[vmem] * 2,
        out_shape=[
            jax.ShapeDtypeStruct((n_coarse, 128), BF16),
            jax.ShapeDtypeStruct((pay_rows, 128), BF16),
        ],
        scratch_shapes=[
            pltpu.VMEM((chunks, n_coarse // chunks, cw), BF16),
            pltpu.VMEM((cw, 256), BF16),
            pltpu.VMEM((n_tok, width), BF16),
            pltpu.SemaphoreType.DMA((3 + chunks,)),
        ],
        compiler_params=pltpu.CompilerParams(vmem_limit_bytes=VMEM_LIMIT),
        cost_estimate=COST,
        name="project",
    )(ids, table, coarse, w_k, w_v, fine)


def query_kernel(ids, kv, pay_o, fine, gain, w_q, pay_e, q_nat, q_t, x_buf, q_buf, sems):
    first = pltpu.make_async_copy(fine, x_buf, sems.at[0])
    second = pltpu.make_async_copy(w_q, q_buf, sems.at[1])
    first.start()
    second.start()
    base = kv.shape[0]
    n_tok, width = x_buf.shape
    half = n_tok // 2
    end = base + half * (width // 128)
    pay_e[0:base, :] = kv[...]
    pay_e[end:, :] = pay_o[end:, :]
    even = lax.rem(ids[0], 2) == 0
    first.wait()
    for c in range(width // 128):
        lanes = slice(128 * c, 128 * c + 128)
        top, bottom = x_buf[0:half, lanes], x_buf[half:, lanes]
        pay_e[base + half * c : base + half * (c + 1), :] = jnp.where(even, bottom, top)
    normed = rms(x_buf[...].astype(F32), gain[...]).astype(BF16)
    second.wait()
    q = jnp.dot(normed, q_buf[...], preferred_element_type=F32) * (1.0 / HD**0.5)
    q_nat[...] = q.astype(BF16)
    q_t[...] = q.T.astype(BF16).reshape(q_t.shape)


def queries(ids, kv, pay_o, fine, gain, w_q):
    n_tok, width = fine.shape
    hbm = pl.BlockSpec(memory_space=pltpu.HBM)
    vmem = pl.BlockSpec(memory_space=pltpu.VMEM)
    return pl.pallas_call(
        query_kernel,
        in_specs=[pl.BlockSpec(memory_space=pltpu.SMEM), vmem, vmem, hbm, vmem, hbm],
        out_specs=[vmem] * 3,
        out_shape=[
            jax.ShapeDtypeStruct(pay_o.shape, BF16),
            jax.ShapeDtypeStruct((n_tok, width), BF16),
            jax.ShapeDtypeStruct((HEADS, HD, n_tok), BF16),
        ],
        scratch_shapes=[
            pltpu.VMEM((n_tok, width), BF16),
            pltpu.VMEM((width, width), BF16),
            pltpu.SemaphoreType.DMA((2,)),
        ],
        compiler_params=pltpu.CompilerParams(vmem_limit_bytes=VMEM_LIMIT),
        cost_estimate=COST,
        name="queries",
    )(ids, kv, pay_o, fine, gain, w_q)


def onward_kernel(ids, got_o, far_on, out):
    out[...] = jnp.where(lax.rem(ids[0], 2) == 0, got_o[0 : out.shape[0], :], far_on[...])


def pass_on(ids, got_o, far_on):
    vmem = pl.BlockSpec(memory_space=pltpu.VMEM)
    return pl.pallas_call(
        onward_kernel,
        in_specs=[pl.BlockSpec(memory_space=pltpu.SMEM), vmem, vmem],
        out_specs=vmem,
        out_shape=jax.ShapeDtypeStruct(far_on.shape, BF16),
        compiler_params=pltpu.CompilerParams(vmem_limit_bytes=VMEM_LIMIT),
        cost_estimate=COST_ONWARD,
        name="pass_on",
    )(ids, got_o, far_on)


def stack_kernel(ids, shifts, base, got_o, got_e, fine, out, rows):
    n_tok, width = fine.shape
    half = n_tok // 2
    even = lax.rem(ids[0], 2) == 0
    rows[half : half + n_tok, :] = fine[...].astype(F32)
    for c in range(width // 128):
        lanes = slice(128 * c, 128 * c + 128)
        at = slice(base + half * c, base + half * (c + 1))
        a, b = got_o[at, :].astype(F32), got_e[at, :].astype(F32)
        rows[0:half, lanes] = jnp.where(even, a, b)
        rows[half + n_tok :, lanes] = jnp.where(even, b, a)
    out[...] = rows[pl.ds(pl.multiple_of(shifts[0] * WS, WS), out.shape[0]), :].astype(BF16)


def stack_rows(ids, shifts, got_o, got_e, fine, base):
    n_tok, width = fine.shape
    vmem = pl.BlockSpec(memory_space=pltpu.VMEM)
    smem = pl.BlockSpec(memory_space=pltpu.SMEM)
    return pl.pallas_call(
        lambda ids, shifts, *refs: stack_kernel(ids, shifts, base, *refs),
        in_specs=[smem, smem] + [vmem] * 3,
        out_specs=vmem,
        out_shape=jax.ShapeDtypeStruct((n_tok + n_tok // 2, width), BF16),
        scratch_shapes=[pltpu.VMEM((2 * n_tok, width), F32)],
        compiler_params=pltpu.CompilerParams(vmem_limit_bytes=VMEM_LIMIT),
        cost_estimate=COST_STACK,
        name="stack_rows",
    )(ids, shifts, got_o, got_e, fine)


def window_kernel(last, ids, shifts, left, mid, right, q, gain, w_k, w_v, out, lse, k_buf, v_buf, sems):
    loads = [pltpu.make_async_copy(w_k, k_buf, sems.at[0]), pltpu.make_async_copy(w_v, v_buf, sems.at[1])]
    for copy in loads:
        copy.start()
    span, width = left.shape
    strip, member = ids[0], ids[1]
    shift_row, shift_col = shifts[0], shifts[1]
    turn = lambda ref: pltpu.roll(ref[...].astype(F32).reshape(span // WS, WS, width), WS - shift_col, 1)
    a, b, c = turn(left), turn(mid), turn(right)
    stays = iota((1, WS, width), 1) < WS - shift_col
    fine = jnp.concatenate([jnp.where(stays, a, b), jnp.where(stays, b, c)], axis=0).reshape(2 * span, width)
    normed = rms(fine, gain[...]).astype(BF16)
    loads[0].wait()
    keys = jnp.dot(normed, k_buf[...], preferred_element_type=F32).astype(BF16)
    loads[1].wait()
    values = jnp.dot(normed, v_buf[...], preferred_element_type=F32).astype(BF16)
    per = 2 * WS * WS
    shape = (128, 2 * per)
    query = lax.rem(iota(shape, 0), 64)
    column_q = lax.rem(query, WS)
    key = iota(shape, 1)
    block = lax.shift_right_arithmetic(key, 7)
    within = lax.bitwise_and(key, per - 1)
    column_k = block * WS - WS + shift_col + lax.bitwise_and(within, WS - 1)
    same_col = (column_q >= shift_col) == (block == 1)
    wrap_col = ((column_k < 0) & (member == 0)) | ((column_k >= WS) & (member == last[1]))
    low = iota((64, 128), 1) < HD
    lane = iota((64, 128), 1)
    own = (iota((128, 128), 0) < 64) == (iota((128, 128), 1) < HD)
    for half in range(2):
        row_q = WS * half + lax.shift_right_arithmetic(query, 3)
        line_k = WS * half + lax.shift_right_arithmetic(within, 3)
        row_k = line_k + shift_row - WS
        same_row = lax.shift_right_arithmetic(row_q - shift_row + WS, 3) == lax.shift_right_arithmetic(line_k, 3)
        wrap_row = ((row_k < 0) & (strip == 0)) | ((row_k >= 2 * WS) & (strip == last[0]))
        seen = same_row & same_col & jnp.logical_not(wrap_row | wrap_col)
        rows = slice(64 * half, 64 * half + 64)
        pick = lambda x: jnp.concatenate(
            [x[span * i + 64 * half : span * i + 64 * half + per] for i in range(2)], axis=0
        )
        keys_h, values_h = pick(keys), pick(values)
        marks = jnp.zeros((64, 128), F32)
        for pair in range(HEADS // 2):
            lanes = slice(128 * pair, 128 * pair + 128)
            q_pair = q[rows, lanes]
            q_both = jnp.concatenate([q_pair, q_pair], axis=0)
            q_both = jnp.where(own, q_both, jnp.zeros_like(q_both))
            score = lax.dot_general(
                q_both, keys_h[:, lanes], (((1,), (1,)), ((), ())), preferred_element_type=F32
            )
            score = jnp.where(seen, score, LOW)
            peak = jnp.max(score, axis=-1, keepdims=True)
            weight = jnp.exp(score - peak)
            total = jnp.sum(weight, axis=-1, keepdims=True)
            mixed = jnp.dot(weight.astype(BF16), values_h[:, lanes], preferred_element_type=F32) / total
            out[rows, lanes] = jnp.where(low, mixed[:64], mixed[64:])
            level = peak + jnp.log(total)
            marks = jnp.where(lane == 2 * pair, level[:64], marks)
            marks = jnp.where(lane == 2 * pair + 1, level[64:], marks)
        lse[rows, :] = marks


def window_attention(ids, shifts, left, mid, right, q, gain, w_k, w_v, last):
    n_tok, width = q.shape
    vmem = pl.BlockSpec(memory_space=pltpu.VMEM)
    smem = pl.BlockSpec(memory_space=pltpu.SMEM)
    return pl.pallas_call(
        lambda *refs: window_kernel(last, *refs),
        in_specs=[smem, smem] + [vmem] * 5 + [pl.BlockSpec(memory_space=pltpu.HBM)] * 2,
        out_specs=[vmem, vmem],
        out_shape=[
            jax.ShapeDtypeStruct((n_tok, width), F32),
            jax.ShapeDtypeStruct((n_tok, 128), F32),
        ],
        scratch_shapes=[
            pltpu.VMEM((width, width), BF16),
            pltpu.VMEM((width, width), BF16),
            pltpu.SemaphoreType.DMA((2,)),
        ],
        compiler_params=pltpu.CompilerParams(vmem_limit_bytes=VMEM_LIMIT),
        cost_estimate=COST,
        name="window_attention",
    )(ids, shifts, left, mid, right, q, gain, w_k, w_v)


def choose_kernel(total, ids, table, table_before, own, got_o, got_e, far, here_out, before_out, here_t, before_t, store):
    n_own = own.shape[0]
    per_strip = n_own // 128
    even = lax.rem(ids[0], 2) == 0
    blocked = lambda ref: ref[0:n_own, :].reshape(per_strip, 128, 128)
    store[0:per_strip] = blocked(far)
    store[2 * per_strip : 3 * per_strip] = blocked(own)

    @pl.when(even)
    def _():
        store[per_strip : 2 * per_strip] = blocked(got_o)
        store[3 * per_strip :] = blocked(got_e)

    @pl.when(jnp.logical_not(even))
    def _():
        store[per_strip : 2 * per_strip] = blocked(got_e)
        store[3 * per_strip :] = blocked(got_o)

    here = [b + per_strip for b in local_blocks(ids, table, per_strip, total)]
    before = [table_before[i] for i in range(table_before.shape[0])]
    for chosen, out, turned in ((here, here_out, here_t), (before, before_out, before_t)):
        for i, b in enumerate(chosen):
            block = store[b]
            at = slice(128 * i, 128 * i + 128)
            out[at, :] = block
            turned[:, at] = block.astype(F32).T.astype(BF16)


def choose_blocks(ids, table, table_before, own, got_o, got_e, far, total):
    vmem = pl.BlockSpec(memory_space=pltpu.VMEM)
    smem = pl.BlockSpec(memory_space=pltpu.SMEM)
    keys = 128 * table.shape[0]
    return pl.pallas_call(
        lambda *refs: choose_kernel(total, *refs),
        in_specs=[smem] * 3 + [vmem] * 4,
        out_specs=[vmem] * 4,
        out_shape=[jax.ShapeDtypeStruct((keys, 128), BF16)] * 2 + [jax.ShapeDtypeStruct((128, keys), BF16)] * 2,
        scratch_shapes=[pltpu.VMEM((4 * own.shape[0] // 128, 128, 128), BF16)],
        compiler_params=pltpu.CompilerParams(vmem_limit_bytes=VMEM_LIMIT),
        cost_estimate=COST_CHOOSE,
        name="choose_blocks",
    )(ids, table, table_before, own, got_o, got_e, far)


def coarse_kernel(after, after_too, shifts, q_t, here_ref, before_ref, here_t_ref, before_t_ref, out):
    kv_here, kv_before, kv_here_t, kv_before_t = here_ref[...], before_ref[...], here_t_ref[...], before_t_ref[...]
    low = iota((1, 128), 1) < 64
    earlier = lax.rem(iota((1, 256), 1), 64) < WS * shifts[0]
    line = iota((16, 256), 0)
    swap = lambda x: pltpu.roll(x, 64, 1)

    def attend(q, mixed_rows):
        q = jnp.concatenate([q, jnp.zeros_like(q)], axis=0)
        score = jnp.dot(kv_here, q, preferred_element_type=F32)
        if mixed_rows:
            score = jnp.where(earlier, jnp.dot(kv_before, q, preferred_element_type=F32), score)
        peak = jnp.max(score, axis=0, keepdims=True)
        weight = jnp.exp(score - peak)
        sums = jnp.sum(weight, axis=0, keepdims=True)
        weight = weight.astype(BF16)
        mixed = jnp.dot(kv_here_t, weight, preferred_element_type=F32)
        if mixed_rows:
            mixed = jnp.where(earlier, jnp.dot(kv_before_t, weight, preferred_element_type=F32), mixed)
        level = peak + jnp.log(sums)
        first = level.astype(BF16).astype(F32)
        second = (level - first).astype(BF16).astype(F32)
        third = level - first - second
        marks = jnp.where(line == 0, first, jnp.where(line == 1, second, jnp.where(line == 2, third, 0.0)))
        return jnp.concatenate([mixed[HD:] / sums, marks], axis=0)

    for group in range(q_t.shape[0] // 4):
        tops, bottoms = [], []
        for pair in range(2):
            a = q_t[4 * group + 2 * pair].astype(F32)
            b = q_t[4 * group + 2 * pair + 1].astype(F32)
            tops.append(jnp.where(low, a, swap(b)).astype(BF16))
            bottoms.append(jnp.where(low, swap(a), b).astype(BF16))
        top = attend(jnp.concatenate(tops, axis=1), True)
        bottom = attend(jnp.concatenate(bottoms, axis=1), False)
        for pair in range(2):
            lanes = slice(128 * pair, 128 * pair + 128)
            t, u = top[:, lanes], bottom[:, lanes]
            out[4 * group + 2 * pair] = jnp.where(low, t, swap(u)).astype(BF16)
            out[4 * group + 2 * pair + 1] = jnp.where(low, swap(t), u).astype(BF16)


def coarse_attention(after, after_too, shifts, q_t, blocks):
    vmem = pl.BlockSpec(memory_space=pltpu.VMEM)
    members, _, n_tok = q_t.shape
    return pl.pallas_call(
        coarse_kernel,
        in_specs=[pl.BlockSpec(memory_space=pl.ANY)] * 2 + [pl.BlockSpec(memory_space=pltpu.SMEM)] + [vmem] * 5,
        out_specs=vmem,
        out_shape=jax.ShapeDtypeStruct((members, HD + 16, n_tok), BF16),
        compiler_params=pltpu.CompilerParams(vmem_limit_bytes=VMEM_LIMIT),
        cost_estimate=COST_COARSE,
        name="coarse_attention",
    )(after, after_too, shifts, q_t, *blocks)


def finish_kernel(
    fine, near, near_lse, coarse, gain, w_out, w_gate, w_up, w_down, out, o_buf, g_buf, u_buf, d_buf, sems
):
    steps, width, chunk = g_buf.shape
    first = pltpu.make_async_copy(w_out, o_buf, sems.at[0])
    first.start()
    loads = []
    for i in range(steps):
        at = pl.ds(chunk * i, chunk)
        loads.append(
            [
                pltpu.make_async_copy(w_gate.at[:, at], g_buf.at[i], sems.at[1 + 3 * i]),
                pltpu.make_async_copy(w_up.at[:, at], u_buf.at[i], sems.at[2 + 3 * i]),
                pltpu.make_async_copy(w_down.at[at], d_buf.at[i], sems.at[3 + 3 * i]),
            ]
        )
        for copy in loads[i]:
            copy.start()
    heads = coarse.shape[0]
    far = jnp.concatenate([coarse[h, 0:HD, :].astype(F32) for h in range(heads)], axis=0).T
    marks = [coarse[h, HD : HD + 16, :].astype(F32) for h in range(heads)]
    level = jnp.concatenate([m[0:1] + m[1:2] + m[2:3] for m in marks], axis=0).T
    diff = near_lse[:, 0:heads] - level
    share = 1.0 / (1.0 + jnp.exp(diff))
    share = jnp.concatenate(
        [jnp.broadcast_to(share[:, h : h + 1], (share.shape[0], HD)) for h in range(heads)], axis=1
    )
    head_out = (near[...] * (1.0 - share) + far * share).astype(BF16)
    first.wait()
    mid = fine[...].astype(F32) + jnp.dot(head_out, o_buf[...], preferred_element_type=F32)
    normed = rms(mid, gain[...]).astype(BF16)
    total = mid
    for i in range(steps):
        loads[i][0].wait()
        gate = jnp.dot(normed, g_buf[i], preferred_element_type=F32)
        loads[i][1].wait()
        up = jnp.dot(normed, u_buf[i], preferred_element_type=F32)
        hidden = (gate * (1.0 / (1.0 + jnp.exp(-gate))) * up).astype(BF16)
        loads[i][2].wait()
        total = total + jnp.dot(hidden, d_buf[i], preferred_element_type=F32)
    out[...] = total.astype(BF16)


def finish(fine, near, near_lse, coarse, gain, w_out, w_gate, w_up, w_down):
    n_tok, width = fine.shape
    ff = w_gate.shape[1]
    chunk = 512
    vmem = pl.BlockSpec(memory_space=pltpu.VMEM)
    hbm = pl.BlockSpec(memory_space=pltpu.HBM)
    return pl.pallas_call(
        finish_kernel,
        in_specs=[vmem] * 5 + [hbm] * 4,
        out_specs=vmem,
        out_shape=jax.ShapeDtypeStruct((n_tok, width), BF16),
        scratch_shapes=[
            pltpu.VMEM((width, width), BF16),
            pltpu.VMEM((ff // chunk, width, chunk), BF16),
            pltpu.VMEM((ff // chunk, width, chunk), BF16),
            pltpu.VMEM((ff // chunk, chunk, width), BF16),
            pltpu.SemaphoreType.DMA((1 + 3 * (ff // chunk),)),
        ],
        compiler_params=pltpu.CompilerParams(vmem_limit_bytes=VMEM_LIMIT),
        cost_estimate=COST,
        name="finish",
    )(fine, near, near_lse, coarse, gain, w_out, w_gate, w_up, w_down)


def local(
    fine,
    coarse,
    block_table,
    shifts,
    attn_gain,
    w_query,
    w_key,
    w_value,
    w_out,
    coarse_key,
    coarse_value,
    mlp_gain,
    w_gate,
    w_up,
    w_down,
):
    strips = lax.axis_size("tile")
    members = lax.axis_size("narrow")
    strip = lax.axis_index("tile").astype(jnp.int32)
    member = lax.axis_index("narrow").astype(jnp.int32)
    ids = jnp.stack([strip, member])
    rows, columns, width = fine.shape
    blocks, block_tokens, cw = coarse.shape
    total = blocks * strips
    n_own = blocks * block_tokens
    flat = fine.reshape(rows * columns, width)
    table = block_table.reshape(-1)
    gain = attn_gain.reshape(1, width)

    stay = lambda x: pltpu.with_memory_space_constraint(x, pltpu.HBM)
    flat_hbm = stay(flat)
    kv, pay_o = project(
        ids, table, stay(coarse.reshape(n_own, cw)), stay(coarse_key), stay(coarse_value), flat_hbm, total
    )
    odd_pairs = [(i, (i - 1) % strips if i % 2 == 0 else (i + 1) % strips) for i in range(strips)]
    even_pairs = [(i, i ^ 1) for i in range(strips)]
    got_o = lax.ppermute(pay_o, "tile", odd_pairs)
    far_on = lax.ppermute(kv, "tile", [(i, (i + 3) % strips) for i in range(0, strips, 2)])
    pay_e, q, q_t = queries(ids, kv, pay_o, flat_hbm, gain, stay(w_query))
    got_e = lax.ppermute(pay_e, "tile", even_pairs)
    q_head = lax.all_to_all(q_t, "narrow", 0, 0, tiled=True)

    onward = pass_on(ids, got_o, far_on)
    onward, got_o, got_e = lax.optimization_barrier((onward, got_o, got_e))
    stacked = stack_rows(ids, shifts, got_o, got_e, flat, n_own)
    stacked, q_head = lax.optimization_barrier((stacked, q_head))
    far = lax.ppermute(onward, "tile", even_pairs)
    right_of = lax.ppermute(stacked, "narrow", [(i, i - 1) for i in range(1, members)])
    left_of = lax.ppermute(stacked, "narrow", [(i, i + 1) for i in range(members - 1)])
    mark_row = n_own + rows * columns // 2 * (width // 128)
    table_before = jnp.where(strip % 2 == 0, got_o[mark_row, :8], got_e[mark_row, :8]).astype(jnp.int32)

    blocks = choose_blocks(ids, table, table_before, kv, got_o, got_e, far, total)
    from_coarse = coarse_attention(left_of, right_of, shifts, q_head, blocks)
    from_coarse = lax.all_to_all(from_coarse, "narrow", 0, 0, tiled=True)
    near, near_lse = window_attention(
        ids, shifts, left_of, stacked, right_of, q, gain, stay(w_key), stay(w_value), (strips - 1, members - 1)
    )
    out = finish(
        flat,
        near,
        near_lse,
        from_coarse,
        mlp_gain.reshape(1, width),
        stay(w_out),
        stay(w_gate),
        stay(w_up),
        stay(w_down),
    )
    return out.reshape(rows, columns, width)


def solution(mesh):
    placed = (
        P("tile", "narrow", None),
        P("tile", None, None),
        P("tile", None),
    ) + (P(),) * 12
    return jax.shard_map(
        local, mesh=mesh, in_specs=placed, out_specs=P("tile", "narrow", None), check_vma=False
    )
```

```python
import jax
import jax.numpy as jnp
from jax import lax
from jax.experimental import pallas as pl
from jax.experimental.pallas import tpu as pltpu
from jax.sharding import PartitionSpec as P

HEADS = 8
HD = 64
WS = 8
HALO = WS - 1
CHUNK = 512
EPS = 1e-06
F32 = jnp.float32
BF16 = jnp.bfloat16
LOW = -1e30
VMEM_LIMIT = 24 * 1024 * 1024
COST = pl.CostEstimate(flops=1000, bytes_accessed=1000, transcendentals=0)
COST_ONWARD = pl.CostEstimate(flops=1000000000, bytes_accessed=1000, transcendentals=0)
COST_STACK = pl.CostEstimate(flops=10000000000, bytes_accessed=1000, transcendentals=0)
COST_HERE = pl.CostEstimate(flops=1000, bytes_accessed=1000, transcendentals=0)
COST_CHOOSE = pl.CostEstimate(flops=10000000000, bytes_accessed=1000, transcendentals=0)


def iota(shape, dim):
    return lax.broadcasted_iota(jnp.int32, shape, dim)


def rms(x, gain):
    mean_square = jnp.mean(x * x, axis=-1, keepdims=True)
    return x * lax.rsqrt(mean_square + EPS) * gain


def local_blocks(ids, table, per_strip, total):
    first = (ids[0] - 1) * per_strip
    return [lax.rem(table[0, i] - first + 2 * total, total) for i in range(table.shape[1])]


def edge_rows(x, top):
    n_tok, width = x.shape
    halo = HALO * WS
    parts = []
    for c in range(width // 128):
        lanes = slice(128 * c, 128 * c + 128)
        first, last = x[0:64, lanes].astype(F32), x[n_tok - 64 :, lanes].astype(F32)
        parts.append(jnp.where(top, first[0:halo], last[64 - halo :]))
    return jnp.concatenate(parts, axis=0).astype(BF16)


def project_kernel(total, ids, table_in, coarse, w_k, w_v, fine, kv, pay_o, table, c_buf, w_buf, x_buf, sems):
    chunks = c_buf.shape[0]
    rows = c_buf.shape[1]
    cols = pl.ds(pl.multiple_of(ids[1] // 2 * 128, 128), 128)
    loads = [
        pltpu.make_async_copy(w_k.at[:, cols], w_buf.at[:, 0:128], sems.at[0]),
        pltpu.make_async_copy(w_v.at[:, cols], w_buf.at[:, 128:256], sems.at[1]),
        pltpu.make_async_copy(fine, x_buf, sems.at[2]),
        pltpu.make_async_copy(table_in, table, sems.at[3 + chunks]),
    ]
    parts = [
        pltpu.make_async_copy(coarse.at[pl.ds(rows * i, rows)], c_buf.at[i], sems.at[3 + i])
        for i in range(chunks)
    ]
    for copy in (loads[0], loads[1], *parts, loads[2], loads[3]):
        copy.start()
    odd_head = lax.rem(ids[1], 2) == 1
    even = lax.rem(ids[0], 2) == 0
    low = iota((rows, 128), 1) < HD
    base = kv.shape[0]
    n_tok, width = x_buf.shape
    half = n_tok // 2
    loads[0].wait()
    loads[1].wait()
    for i in range(chunks):
        parts[i].wait()
        tokens = c_buf[i]
        product = jnp.dot(tokens, w_buf[...], preferred_element_type=F32)
        key, value = product[:, 0:128], product[:, 128:256]
        key = jnp.where(odd_head, pltpu.roll(key, HD, 1), key)
        value = jnp.where(odd_head, value, pltpu.roll(value, HD, 1))
        both = jnp.where(low, key, value).astype(BF16)
        at = slice(rows * i, rows * i + rows)
        kv[at, :] = both
        pay_o[at, :] = both
    loads[3].wait()
    chosen = local_blocks(ids, table, base // 128, total)
    lane = iota((16, 128), 1)
    marks = jnp.zeros((16, 128), F32)
    for i, b in enumerate(chosen):
        marks = jnp.where(lane == i, b.astype(F32), marks)
    end = base + HALO * WS * (width // 128)
    pay_o[end : end + 16, :] = marks.astype(BF16)
    loads[2].wait()
    pay_o[base:end, :] = edge_rows(x_buf, even)


def project(ids, table, coarse, w_k, w_v, fine, total):
    n_coarse, cw = coarse.shape
    n_tok, width = fine.shape
    chunks = 2
    pay_rows = n_coarse + HALO * WS * (width // 128) + 16
    smem = pl.BlockSpec(memory_space=pltpu.SMEM)
    hbm = pl.BlockSpec(memory_space=pltpu.HBM)
    vmem = pl.BlockSpec(memory_space=pltpu.VMEM)
    return pl.pallas_call(
        lambda *refs: project_kernel(total, *refs),
        in_specs=[smem] + [hbm] * 5,
        out_specs=[vmem] * 2,
        out_shape=[
            jax.ShapeDtypeStruct((n_coarse, 128), BF16),
            jax.ShapeDtypeStruct((pay_rows, 128), BF16),
        ],
        scratch_shapes=[
            pltpu.SMEM(table.shape, jnp.int32),
            pltpu.VMEM((chunks, n_coarse // chunks, cw), BF16),
            pltpu.VMEM((cw, 256), BF16),
            pltpu.VMEM((n_tok, width), BF16),
            pltpu.SemaphoreType.DMA((4 + chunks,)),
        ],
        compiler_params=pltpu.CompilerParams(vmem_limit_bytes=VMEM_LIMIT),
        cost_estimate=COST,
        name="project",
    )(ids, table, coarse, w_k, w_v, fine)


def query_kernel(ids, kv, pay_o, fine, gain, w_q, pay_e, q_nat, q_t, x_buf, q_buf, sems):
    first = pltpu.make_async_copy(fine, x_buf, sems.at[0])
    second = pltpu.make_async_copy(w_q, q_buf, sems.at[1])
    first.start()
    second.start()
    base = kv.shape[0]
    n_tok, width = x_buf.shape
    halo = HALO * WS
    end = base + halo * (width // 128)
    pay_e[0:base, :] = kv[...]
    pay_e[end:, :] = pay_o[end:, :]
    even = lax.rem(ids[0], 2) == 0
    first.wait()
    pay_e[base:end, :] = edge_rows(x_buf, jnp.logical_not(even))
    normed = rms(x_buf[...].astype(F32), gain[...]).astype(BF16)
    second.wait()
    q = jnp.dot(normed, q_buf[...], preferred_element_type=F32) * (1.0 / HD**0.5)
    q_nat[...] = q.astype(BF16)
    q_t[...] = q.T.astype(BF16).reshape(q_t.shape)


def queries(ids, kv, pay_o, fine, gain, w_q):
    n_tok, width = fine.shape
    hbm = pl.BlockSpec(memory_space=pltpu.HBM)
    vmem = pl.BlockSpec(memory_space=pltpu.VMEM)
    return pl.pallas_call(
        query_kernel,
        in_specs=[pl.BlockSpec(memory_space=pltpu.SMEM), vmem, vmem, hbm, vmem, hbm],
        out_specs=[vmem] * 3,
        out_shape=[
            jax.ShapeDtypeStruct(pay_o.shape, BF16),
            jax.ShapeDtypeStruct((n_tok, width), BF16),
            jax.ShapeDtypeStruct((HEADS, HD, n_tok), BF16),
        ],
        scratch_shapes=[
            pltpu.VMEM((n_tok, width), BF16),
            pltpu.VMEM((width, width), BF16),
            pltpu.SemaphoreType.DMA((2,)),
        ],
        compiler_params=pltpu.CompilerParams(vmem_limit_bytes=VMEM_LIMIT),
        cost_estimate=COST,
        name="queries",
    )(ids, kv, pay_o, fine, gain, w_q)


def onward_kernel(ids, got_o, far_on, out):
    out[...] = jnp.where(lax.rem(ids[0], 2) == 0, got_o[0 : out.shape[0], :], far_on[...])


def pass_on(ids, got_o, far_on):
    vmem = pl.BlockSpec(memory_space=pltpu.VMEM)
    return pl.pallas_call(
        onward_kernel,
        in_specs=[pl.BlockSpec(memory_space=pltpu.SMEM), vmem, vmem],
        out_specs=vmem,
        out_shape=jax.ShapeDtypeStruct(far_on.shape, BF16),
        compiler_params=pltpu.CompilerParams(vmem_limit_bytes=VMEM_LIMIT),
        cost_estimate=COST_ONWARD,
        name="pass_on",
    )(ids, got_o, far_on)


def stack_kernel(ids, shifts, base, got_o, got_e, fine, out, rows):
    n_tok, width = fine.shape
    half = n_tok // 2
    even = lax.rem(ids[0], 2) == 0
    rows[half : half + n_tok, :] = fine[...].astype(F32)
    halo = HALO * WS
    end = base + halo * (width // 128)
    a, b = got_o[base:end, :].astype(F32), got_e[base:end, :].astype(F32)
    above, below = jnp.where(even, a, b), jnp.where(even, b, a)
    for c in range(width // 128):
        lanes = slice(128 * c, 128 * c + 128)
        at = slice(halo * c, halo * c + halo)
        rows[half - halo : half, lanes] = above[at]
        rows[half + n_tok : half + n_tok + halo, lanes] = below[at]
    out[...] = rows[pl.ds(pl.multiple_of(shifts[0] * WS, WS), out.shape[0]), :].astype(BF16)


def stack_rows(ids, shifts, got_o, got_e, fine, base):
    n_tok, width = fine.shape
    vmem = pl.BlockSpec(memory_space=pltpu.VMEM)
    smem = pl.BlockSpec(memory_space=pltpu.SMEM)
    return pl.pallas_call(
        lambda ids, shifts, *refs: stack_kernel(ids, shifts, base, *refs),
        in_specs=[smem, smem] + [vmem] * 3,
        out_specs=vmem,
        out_shape=jax.ShapeDtypeStruct((n_tok + n_tok // 2, width), BF16),
        scratch_shapes=[pltpu.VMEM((2 * n_tok, width), F32)],
        compiler_params=pltpu.CompilerParams(vmem_limit_bytes=VMEM_LIMIT),
        cost_estimate=COST_STACK,
        name="stack_rows",
    )(ids, shifts, got_o, got_e, fine)


def window_kernel(last, count, ids, shifts, left, mid, right, q, gain, w_k, w_v, *refs):
    weights, (out, lse), held = refs[:count], refs[count : count + 2], refs[count + 2 : 2 * count + 2]
    k_buf, v_buf, sems = refs[2 * count + 2 :]
    loads = [pltpu.make_async_copy(w_k, k_buf, sems.at[0]), pltpu.make_async_copy(w_v, v_buf, sems.at[1])]
    for copy in loads:
        copy.start()
    early = [
        pltpu.make_async_copy(w.at[0 : h.shape[0], 0 : h.shape[1]], h, sems.at[2 + i])
        for i, (w, h) in enumerate(zip(weights, held))
    ]
    span, width = left.shape
    strip, member = ids[0], ids[1]
    shift_row, shift_col = shifts[0], shifts[1]
    turn = lambda ref: pltpu.roll(ref[...].astype(F32).reshape(span // WS, WS, width), WS - shift_col, 1)
    a, b, c = turn(left), turn(mid), turn(right)
    stays = iota((1, WS, width), 1) < WS - shift_col
    fine = jnp.concatenate([jnp.where(stays, a, b), jnp.where(stays, b, c)], axis=0).reshape(2 * span, width)
    normed = rms(fine, gain[...]).astype(BF16)
    loads[0].wait()
    keys = jnp.dot(normed, k_buf[...], preferred_element_type=F32).astype(BF16)
    loads[1].wait()
    for copy in early:
        copy.start()
    values = jnp.dot(normed, v_buf[...], preferred_element_type=F32).astype(BF16)
    per = 2 * WS * WS
    shape = (128, 2 * per)
    query = lax.rem(iota(shape, 0), 64)
    column_q = lax.rem(query, WS)
    key = iota(shape, 1)
    block = lax.shift_right_arithmetic(key, 7)
    within = lax.bitwise_and(key, per - 1)
    column_k = block * WS - WS + shift_col + lax.bitwise_and(within, WS - 1)
    same_col = (column_q >= shift_col) == (block == 1)
    wrap_col = ((column_k < 0) & (member == 0)) | ((column_k >= WS) & (member == last[1]))
    low = iota((64, 128), 1) < HD
    lane = iota((64, 128), 1)
    own = (iota((128, 128), 0) < 64) == (iota((128, 128), 1) < HD)
    for half in range(2):
        row_q = WS * half + lax.shift_right_arithmetic(query, 3)
        line_k = WS * half + lax.shift_right_arithmetic(within, 3)
        row_k = line_k + shift_row - WS
        same_row = lax.shift_right_arithmetic(row_q - shift_row + WS, 3) == lax.shift_right_arithmetic(line_k, 3)
        wrap_row = ((row_k < 0) & (strip == 0)) | ((row_k >= 2 * WS) & (strip == last[0]))
        seen = same_row & same_col & jnp.logical_not(wrap_row | wrap_col)
        rows = slice(64 * half, 64 * half + 64)
        pick = lambda x: jnp.concatenate(
            [x[span * i + 64 * half : span * i + 64 * half + per] for i in range(2)], axis=0
        )
        keys_h, values_h = pick(keys), pick(values)
        marks = jnp.zeros((64, 128), F32)
        for pair in range(HEADS // 2):
            lanes = slice(128 * pair, 128 * pair + 128)
            q_pair = q[rows, lanes]
            q_both = jnp.concatenate([q_pair, q_pair], axis=0)
            q_both = jnp.where(own, q_both, jnp.zeros_like(q_both))
            score = lax.dot_general(
                q_both, keys_h[:, lanes], (((1,), (1,)), ((), ())), preferred_element_type=F32
            )
            score = jnp.where(seen, score, LOW)
            peak = jnp.max(score, axis=-1, keepdims=True)
            weight = jnp.exp(score - peak)
            total = jnp.sum(weight, axis=-1, keepdims=True)
            mixed = jnp.dot(weight.astype(BF16), values_h[:, lanes], preferred_element_type=F32) / total
            out[rows, lanes] = jnp.where(low, mixed[:64], mixed[64:])
            level = peak + jnp.log(total)
            marks = jnp.where(lane == 2 * pair, level[:64], marks)
            marks = jnp.where(lane == 2 * pair + 1, level[64:], marks)
        lse[rows, :] = marks
    for copy in early:
        copy.wait()


def window_attention(ids, shifts, left, mid, right, q, gain, w_k, w_v, weights, last):
    n_tok, width = q.shape
    count = len(weights)
    vmem = pl.BlockSpec(memory_space=pltpu.VMEM)
    smem = pl.BlockSpec(memory_space=pltpu.SMEM)
    return pl.pallas_call(
        lambda *refs: window_kernel(last, count, *refs),
        in_specs=[smem, smem] + [vmem] * 5 + [pl.BlockSpec(memory_space=pltpu.HBM)] * (2 + count),
        out_specs=[vmem] * (2 + count),
        out_shape=[
            jax.ShapeDtypeStruct((n_tok, width), F32),
            jax.ShapeDtypeStruct((n_tok, 128), F32),
        ]
        + [jax.ShapeDtypeStruct((min(w.shape[0], CHUNK), min(w.shape[1], CHUNK)), w.dtype) for w in weights],
        scratch_shapes=[
            pltpu.VMEM((width, width), BF16),
            pltpu.VMEM((width, width), BF16),
            pltpu.SemaphoreType.DMA((2 + count,)),
        ],
        compiler_params=pltpu.CompilerParams(vmem_limit_bytes=VMEM_LIMIT),
        cost_estimate=COST,
        name="window_attention",
    )(ids, shifts, left, mid, right, q, gain, w_k, w_v, *weights)


def attend(q, kv, kv_t):
    score = jnp.dot(kv, jnp.concatenate([q, jnp.zeros_like(q)], axis=0), preferred_element_type=F32)
    peak = jnp.max(score, axis=0, keepdims=True)
    weight = jnp.exp(score - peak)
    sums = jnp.sum(weight, axis=0, keepdims=True)
    mixed = jnp.dot(kv_t, weight.astype(BF16), preferred_element_type=F32)
    level = peak + jnp.log(sums)
    first = level.astype(BF16).astype(F32)
    second = (level - first).astype(BF16).astype(F32)
    third = level - first - second
    line = iota((16, q.shape[1]), 0)
    marks = jnp.where(line == 0, first, jnp.where(line == 1, second, jnp.where(line == 2, third, 0.0)))
    return jnp.concatenate([mixed[HD:] / sums, marks], axis=0)


def swap_halves(x):
    return pltpu.roll(x, 64, 1)


def top_rows(q_t, group):
    low = iota((1, 128), 1) < 64
    tiles = []
    for pair in range(2):
        a, b = (q_t[4 * group + 2 * pair + k].astype(F32) for k in range(2))
        tiles.append(jnp.where(low, a, swap_halves(b)).astype(BF16))
    return jnp.concatenate(tiles, axis=1)


def bottom_rows(q_t, group):
    low = iota((1, 128), 1) < 64
    tiles = []
    for pair in range(2):
        a, b = (q_t[4 * group + 2 * pair + k].astype(F32) for k in range(2))
        tiles.append(jnp.where(low, swap_halves(a), b).astype(BF16))
    return jnp.concatenate(tiles, axis=1)


def here_kernel(total, ids, table, q_t, own, got_o, got_e, out, store, turned):
    n_own = own.shape[0]
    per_strip = n_own // 128
    even = lax.rem(ids[0], 2) == 0
    blocked = lambda ref: ref[0:n_own, :].reshape(per_strip, 128, 128)
    above, below = blocked(got_o), blocked(got_e)
    store[0:per_strip] = jnp.where(even, above, below)
    store[per_strip : 2 * per_strip] = blocked(own)
    store[2 * per_strip :] = jnp.where(even, below, above)
    chosen = local_blocks(ids, table, per_strip, total)
    kv = jnp.concatenate([store[b] for b in chosen], axis=0)
    turned[...] = kv.astype(F32).T.astype(BF16)
    kv_t = turned[...]
    low = iota((1, 128), 1) < 64
    for group in range(q_t.shape[0] // 4):
        top = attend(top_rows(q_t, group), kv, kv_t)
        bottom = attend(bottom_rows(q_t, group), kv, kv_t)
        for pair in range(2):
            lanes = slice(128 * pair, 128 * pair + 128)
            t, u = top[:, lanes], bottom[:, lanes]
            out[4 * group + 2 * pair] = jnp.where(low, t, swap_halves(u)).astype(BF16)
            out[4 * group + 2 * pair + 1] = jnp.where(low, swap_halves(t), u).astype(BF16)


def here_attention(ids, table, q_t, own, got_o, got_e, total):
    vmem = pl.BlockSpec(memory_space=pltpu.VMEM)
    smem = pl.BlockSpec(memory_space=pltpu.SMEM)
    members, _, n_tok = q_t.shape
    return pl.pallas_call(
        lambda *refs: here_kernel(total, *refs),
        in_specs=[smem, smem] + [vmem] * 4,
        out_specs=vmem,
        out_shape=jax.ShapeDtypeStruct((members, HD + 16, n_tok), BF16),
        scratch_shapes=[
            pltpu.VMEM((3 * own.shape[0] // 128, 128, 128), BF16),
            pltpu.VMEM((128, 128 * table.shape[1]), BF16),
        ],
        compiler_params=pltpu.CompilerParams(vmem_limit_bytes=VMEM_LIMIT),
        cost_estimate=COST_HERE,
        name="here_attention",
    )(ids, table, q_t, own, got_o, got_e)


def choose_kernel(after, ids, table, far, got_o, got_e, own, kv, kv_t, store):
    n_own = own.shape[0]
    per_strip = n_own // 128
    even = lax.rem(ids[0], 2) == 0
    blocked = lambda ref: ref[0:n_own, :].reshape(per_strip, 128, 128)
    store[0:per_strip] = blocked(far)
    store[per_strip : 2 * per_strip] = jnp.where(even, blocked(got_o), blocked(got_e))
    store[2 * per_strip :] = blocked(own)
    for i in range(table.shape[0]):
        block = store[table[i]]
        at = slice(128 * i, 128 * i + 128)
        kv[at, :] = block
        kv_t[:, at] = block.astype(F32).T.astype(BF16)


def choose_blocks(after, ids, table, far, got_o, got_e, own):
    vmem = pl.BlockSpec(memory_space=pltpu.VMEM)
    smem = pl.BlockSpec(memory_space=pltpu.SMEM)
    keys = 128 * table.shape[0]
    return pl.pallas_call(
        choose_kernel,
        in_specs=[pl.BlockSpec(memory_space=pl.ANY), smem, smem] + [vmem] * 4,
        out_specs=[vmem] * 2,
        out_shape=[jax.ShapeDtypeStruct((keys, 128), BF16), jax.ShapeDtypeStruct((128, keys), BF16)],
        scratch_shapes=[pltpu.VMEM((3 * own.shape[0] // 128, 128, 128), BF16)],
        compiler_params=pltpu.CompilerParams(vmem_limit_bytes=VMEM_LIMIT),
        cost_estimate=COST_CHOOSE,
        name="choose_blocks",
    )(after, ids, table, far, got_o, got_e, own)


def before_kernel(after, after_too, shifts, q_t, kv, kv_t, here, out):
    lane = iota((1, 128), 1)
    earlier = lane < WS * shifts[0]
    for group in range(q_t.shape[0] // 4):
        top = attend(top_rows(q_t, group), kv[...], kv_t[...])
        for pair in range(2):
            t = top[:, 128 * pair : 128 * pair + 128]
            for k in range(2):
                m = 4 * group + 2 * pair + k
                mine = t if k == 0 else swap_halves(t)
                out[m] = jnp.where(earlier, mine, here[m].astype(F32)).astype(BF16)


def before_attention(after, after_too, shifts, q_t, kv, kv_t, here):
    vmem = pl.BlockSpec(memory_space=pltpu.VMEM)
    return pl.pallas_call(
        before_kernel,
        in_specs=[pl.BlockSpec(memory_space=pl.ANY)] * 2 + [pl.BlockSpec(memory_space=pltpu.SMEM)] + [vmem] * 4,
        out_specs=vmem,
        out_shape=jax.ShapeDtypeStruct(here.shape, BF16),
        compiler_params=pltpu.CompilerParams(vmem_limit_bytes=VMEM_LIMIT),
        cost_estimate=COST,
        name="before_attention",
    )(after, after_too, shifts, q_t, kv, kv_t, here)


def finish_kernel(
    fine, near, near_lse, coarse, gain, w_out, gate_0, up_0, down_0, w_gate, w_up, w_down, out, g_buf, u_buf, d_buf, sems
):
    steps = w_gate.shape[1] // CHUNK
    loads = []
    for i in range(1, steps):
        at = pl.ds(CHUNK * i, CHUNK)
        loads.append(
            [
                pltpu.make_async_copy(w_gate.at[:, at], g_buf.at[i - 1], sems.at[3 * i - 3]),
                pltpu.make_async_copy(w_up.at[:, at], u_buf.at[i - 1], sems.at[3 * i - 2]),
                pltpu.make_async_copy(w_down.at[at], d_buf.at[i - 1], sems.at[3 * i - 1]),
            ]
        )
    for group in loads:
        for copy in group:
            copy.start()
    heads = coarse.shape[0]
    far = jnp.concatenate([coarse[h, 0:HD, :].astype(F32) for h in range(heads)], axis=0).T
    marks = [coarse[h, HD : HD + 16, :].astype(F32) for h in range(heads)]
    level = jnp.concatenate([m[0:1] + m[1:2] + m[2:3] for m in marks], axis=0).T
    diff = near_lse[:, 0:heads] - level
    share = 1.0 / (1.0 + jnp.exp(diff))
    share = jnp.concatenate(
        [jnp.broadcast_to(share[:, h : h + 1], (share.shape[0], HD)) for h in range(heads)], axis=1
    )
    head_out = (near[...] * (1.0 - share) + far * share).astype(BF16)
    mid = fine[...].astype(F32) + jnp.dot(head_out, w_out[...], preferred_element_type=F32)
    normed = rms(mid, gain[...]).astype(BF16)
    total = mid
    for i in range(steps):
        if i == 0:
            parts = (gate_0, up_0, down_0)
        else:
            for copy in loads[i - 1]:
                copy.wait()
            parts = (g_buf.at[i - 1], u_buf.at[i - 1], d_buf.at[i - 1])
        gate = jnp.dot(normed, parts[0][...], preferred_element_type=F32)
        up = jnp.dot(normed, parts[1][...], preferred_element_type=F32)
        hidden = (gate * (1.0 / (1.0 + jnp.exp(-gate))) * up).astype(BF16)
        total = total + jnp.dot(hidden, parts[2][...], preferred_element_type=F32)
    out[...] = total.astype(BF16)


def finish(fine, near, near_lse, coarse, gain, w_out, gate_0, up_0, down_0, w_gate, w_up, w_down):
    n_tok, width = fine.shape
    rest = w_gate.shape[1] // CHUNK - 1
    vmem = pl.BlockSpec(memory_space=pltpu.VMEM)
    hbm = pl.BlockSpec(memory_space=pltpu.HBM)
    return pl.pallas_call(
        finish_kernel,
        in_specs=[vmem] * 9 + [hbm] * 3,
        out_specs=vmem,
        out_shape=jax.ShapeDtypeStruct((n_tok, width), BF16),
        scratch_shapes=[
            pltpu.VMEM((rest, width, CHUNK), BF16),
            pltpu.VMEM((rest, width, CHUNK), BF16),
            pltpu.VMEM((rest, CHUNK, width), BF16),
            pltpu.SemaphoreType.DMA((3 * rest,)),
        ],
        compiler_params=pltpu.CompilerParams(vmem_limit_bytes=VMEM_LIMIT),
        cost_estimate=COST,
        name="finish",
    )(fine, near, near_lse, coarse, gain, w_out, gate_0, up_0, down_0, w_gate, w_up, w_down)


def local(
    fine,
    coarse,
    block_table,
    shifts,
    attn_gain,
    w_query,
    w_key,
    w_value,
    w_out,
    coarse_key,
    coarse_value,
    mlp_gain,
    w_gate,
    w_up,
    w_down,
):
    strips = lax.axis_size("tile")
    members = lax.axis_size("narrow")
    strip = lax.axis_index("tile").astype(jnp.int32)
    member = lax.axis_index("narrow").astype(jnp.int32)
    ids = jnp.stack([strip, member])
    rows, columns, width = fine.shape
    blocks, block_tokens, cw = coarse.shape
    total = blocks * strips
    n_own = blocks * block_tokens
    flat = fine.reshape(rows * columns, width)
    table = block_table
    gain = attn_gain.reshape(1, width)

    stay = lambda x: pltpu.with_memory_space_constraint(x, pltpu.HBM)
    flat_hbm = stay(flat)
    kv, pay_o = project(
        ids, stay(table), stay(coarse.reshape(n_own, cw)), stay(coarse_key), stay(coarse_value), flat_hbm, total
    )
    odd_pairs = [(i, (i - 1) % strips if i % 2 == 0 else (i + 1) % strips) for i in range(strips)]
    even_pairs = [(i, i ^ 1) for i in range(strips)]
    got_o = lax.ppermute(pay_o, "tile", odd_pairs)
    far_on = lax.ppermute(kv, "tile", [(i, (i + 3) % strips) for i in range(0, strips, 2)])
    pay_e, q, q_t = queries(ids, kv, pay_o, flat_hbm, gain, stay(w_query))
    got_e = lax.ppermute(pay_e, "tile", even_pairs)
    q_head = lax.all_to_all(q_t, "narrow", 0, 0, tiled=True)

    onward = pass_on(ids, got_o, far_on)
    onward, got_o, got_e = lax.optimization_barrier((onward, got_o, got_e))
    stacked = stack_rows(ids, shifts, got_o, got_e, flat, n_own)
    stacked, q_head = lax.optimization_barrier((stacked, q_head))
    far = lax.ppermute(onward, "tile", even_pairs)
    right_of = lax.ppermute(stacked, "narrow", [(i, i - 1) for i in range(1, members)])
    left_of = lax.ppermute(stacked, "narrow", [(i, i + 1) for i in range(members - 1)])
    mark_row = n_own + HALO * WS * (width // 128)
    table_before = jnp.where(strip % 2 == 0, got_o[mark_row, :8], got_e[mark_row, :8]).astype(jnp.int32)

    here = here_attention(ids, table, q_head, kv, got_o, got_e, total)
    kv_before, kv_before_t = choose_blocks(here, ids, table_before, far, got_o, got_e, kv)
    from_coarse = before_attention(left_of, right_of, shifts, q_head, kv_before, kv_before_t, here)
    from_coarse = lax.all_to_all(from_coarse, "narrow", 0, 0, tiled=True)
    near, near_lse, *held = window_attention(
        ids,
        shifts,
        left_of,
        stacked,
        right_of,
        q,
        gain,
        stay(w_key),
        stay(w_value),
        (stay(w_out), stay(w_gate), stay(w_up), stay(w_down)),
        (strips - 1, members - 1),
    )
    out = finish(
        flat,
        near,
        near_lse,
        from_coarse,
        mlp_gain.reshape(1, width),
        *held,
        stay(w_gate),
        stay(w_up),
        stay(w_down),
    )
    return out.reshape(rows, columns, width)


def solution(mesh):
    placed = (
        P("tile", "narrow", None),
        P("tile", None, None),
        P("tile", None),
    ) + (P(),) * 12
    return jax.shard_map(
        local, mesh=mesh, in_specs=placed, out_specs=P("tile", "narrow", None), check_vma=False
    )
```

```python
import jax
import jax.numpy as jnp
from jax import lax
from jax.experimental import pallas as pl
from jax.experimental.pallas import tpu as pltpu
from jax.sharding import PartitionSpec as P

HEADS = 8
HD = 64
WS = 8
HALO = WS - 1
PLANE = 16
CHUNK = 512
EPS = 1e-06
F32 = jnp.float32
BF16 = jnp.bfloat16
LOW = -1e30
VMEM_LIMIT = 24 * 1024 * 1024
COST = pl.CostEstimate(flops=1000, bytes_accessed=1000, transcendentals=0)
COST_STACK = pl.CostEstimate(flops=10000000000, bytes_accessed=1000, transcendentals=0)
COST_HERE = pl.CostEstimate(flops=1000, bytes_accessed=1000, transcendentals=0)
COST_CHOOSE = pl.CostEstimate(flops=10000000000, bytes_accessed=1000, transcendentals=0)


def iota(shape, dim):
    return lax.broadcasted_iota(jnp.int32, shape, dim)


def rms(x, gain):
    mean_square = jnp.mean(x * x, axis=-1, keepdims=True)
    return x * lax.rsqrt(mean_square + EPS) * gain


def local_blocks(ids, table, per_strip, total):
    first = (ids[0] - 1) * per_strip
    return [lax.rem(table[0, i] - first + 2 * total, total) for i in range(table.shape[1])]


def edge_rows(x, top):
    n_tok, width = x.shape
    halo = HALO * WS
    parts = []
    for c in range(width // 128):
        lanes = slice(128 * c, 128 * c + 128)
        first, last = x[0:64, lanes].astype(F32), x[n_tok - 64 :, lanes].astype(F32)
        parts.append(jnp.where(top, first[0:halo], last[64 - halo :]))
    return jnp.concatenate(parts, axis=0).astype(BF16)


def project_kernel(total, ids, table_in, coarse, w_k, w_v, fine, kv, pay_o, pay_e, table, c_buf, w_buf, x_buf, sems):
    chunks = c_buf.shape[0]
    rows = c_buf.shape[1]
    cols = pl.ds(pl.multiple_of(ids[1] // 2 * 128, 128), 128)
    loads = [
        pltpu.make_async_copy(w_k.at[:, cols], w_buf.at[:, 0:128], sems.at[0]),
        pltpu.make_async_copy(w_v.at[:, cols], w_buf.at[:, 128:256], sems.at[1]),
        pltpu.make_async_copy(fine, x_buf, sems.at[2]),
        pltpu.make_async_copy(table_in, table, sems.at[3 + chunks]),
    ]
    parts = [
        pltpu.make_async_copy(coarse.at[pl.ds(rows * i, rows)], c_buf.at[i], sems.at[3 + i])
        for i in range(chunks)
    ]
    for copy in (loads[0], loads[1], *parts, loads[2], loads[3]):
        copy.start()
    odd_head = lax.rem(ids[1], 2) == 1
    even = lax.rem(ids[0], 2) == 0
    low = iota((rows, 128), 1) < HD
    base = kv.shape[0]
    n_tok, width = x_buf.shape
    half = n_tok // 2
    loads[0].wait()
    loads[1].wait()
    for i in range(chunks):
        parts[i].wait()
        tokens = c_buf[i]
        product = jnp.dot(tokens, w_buf[...], preferred_element_type=F32)
        key, value = product[:, 0:128], product[:, 128:256]
        key = jnp.where(odd_head, pltpu.roll(key, HD, 1), key)
        value = jnp.where(odd_head, value, pltpu.roll(value, HD, 1))
        both = jnp.where(low, key, value).astype(BF16)
        at = slice(rows * i, rows * i + rows)
        kv[at, :] = both
        pay_o[at, :] = both
        pay_e[at, :] = both
    loads[3].wait()
    chosen = local_blocks(ids, table, base // 128, total)
    lane = iota((16, 128), 1)
    marks = jnp.zeros((16, 128), F32)
    for i, b in enumerate(chosen):
        marks = jnp.where(lane == i, b.astype(F32), marks)
    end = base + HALO * WS * (width // 128)
    pay_o[end : end + 16, :] = marks.astype(BF16)
    pay_e[end : end + 16, :] = marks.astype(BF16)
    loads[2].wait()
    pay_o[base:end, :] = edge_rows(x_buf, even)
    pay_e[base:end, :] = edge_rows(x_buf, jnp.logical_not(even))


def project(ids, table, coarse, w_k, w_v, fine, total):
    n_coarse, cw = coarse.shape
    n_tok, width = fine.shape
    chunks = 2
    pay_rows = n_coarse + HALO * WS * (width // 128) + 16
    smem = pl.BlockSpec(memory_space=pltpu.SMEM)
    hbm = pl.BlockSpec(memory_space=pltpu.HBM)
    vmem = pl.BlockSpec(memory_space=pltpu.VMEM)
    return pl.pallas_call(
        lambda *refs: project_kernel(total, *refs),
        in_specs=[smem] + [hbm] * 5,
        out_specs=[vmem] * 3,
        out_shape=[
            jax.ShapeDtypeStruct((n_coarse, 128), BF16),
            jax.ShapeDtypeStruct((pay_rows, 128), BF16),
            jax.ShapeDtypeStruct((pay_rows, 128), BF16),
        ],
        scratch_shapes=[
            pltpu.SMEM(table.shape, jnp.int32),
            pltpu.VMEM((chunks, n_coarse // chunks, cw), BF16),
            pltpu.VMEM((cw, 256), BF16),
            pltpu.VMEM((n_tok, width), BF16),
            pltpu.SemaphoreType.DMA((4 + chunks,)),
        ],
        compiler_params=pltpu.CompilerParams(vmem_limit_bytes=VMEM_LIMIT),
        cost_estimate=COST,
        name="project",
    )(ids, table, coarse, w_k, w_v, fine)


def query_kernel(after, fine, gain, w_q, q_nat, q_t, x_buf, q_buf, sems):
    first = pltpu.make_async_copy(fine, x_buf, sems.at[0])
    second = pltpu.make_async_copy(w_q, q_buf, sems.at[1])
    first.start()
    second.start()
    first.wait()
    normed = rms(x_buf[...].astype(F32), gain[...]).astype(BF16)
    second.wait()
    q = jnp.dot(normed, q_buf[...], preferred_element_type=F32) * (1.0 / HD**0.5)
    q_nat[...] = q.astype(BF16)
    q_t[...] = q.T.astype(BF16).reshape(q_t.shape)


def queries(after, fine, gain, w_q):
    n_tok, width = fine.shape
    hbm = pl.BlockSpec(memory_space=pltpu.HBM)
    vmem = pl.BlockSpec(memory_space=pltpu.VMEM)
    return pl.pallas_call(
        query_kernel,
        in_specs=[pl.BlockSpec(memory_space=pl.ANY), hbm, vmem, hbm],
        out_specs=[vmem] * 2,
        out_shape=[
            jax.ShapeDtypeStruct((n_tok, width), BF16),
            jax.ShapeDtypeStruct((HEADS, HD, n_tok), BF16),
        ],
        scratch_shapes=[
            pltpu.VMEM((n_tok, width), BF16),
            pltpu.VMEM((width, width), BF16),
            pltpu.SemaphoreType.DMA((2,)),
        ],
        compiler_params=pltpu.CompilerParams(vmem_limit_bytes=VMEM_LIMIT),
        cost_estimate=COST,
        name="queries",
    )(after, fine, gain, w_q)


def stack_kernel(ids, shifts, base, got_o, got_e, fine, out, rows):
    n_tok, width = fine.shape
    half = n_tok // 2
    even = lax.rem(ids[0], 2) == 0
    rows[half : half + n_tok, :] = fine[...].astype(F32)
    halo = HALO * WS
    end = base + halo * (width // 128)
    a, b = got_o[base:end, :].astype(F32), got_e[base:end, :].astype(F32)
    above, below = jnp.where(even, a, b), jnp.where(even, b, a)
    for c in range(width // 128):
        lanes = slice(128 * c, 128 * c + 128)
        at = slice(halo * c, halo * c + halo)
        rows[half - halo : half, lanes] = above[at]
        rows[half + n_tok : half + n_tok + halo, lanes] = below[at]
    out[...] = rows[pl.ds(pl.multiple_of(shifts[0] * WS, WS), out.shape[0]), :].astype(BF16)


def stack_rows(ids, shifts, got_o, got_e, fine, base):
    n_tok, width = fine.shape
    vmem = pl.BlockSpec(memory_space=pltpu.VMEM)
    smem = pl.BlockSpec(memory_space=pltpu.SMEM)
    return pl.pallas_call(
        lambda ids, shifts, *refs: stack_kernel(ids, shifts, base, *refs),
        in_specs=[smem, smem] + [vmem] * 3,
        out_specs=vmem,
        out_shape=jax.ShapeDtypeStruct((n_tok + n_tok // 2, width), BF16),
        scratch_shapes=[pltpu.VMEM((2 * n_tok, width), F32)],
        compiler_params=pltpu.CompilerParams(vmem_limit_bytes=VMEM_LIMIT),
        cost_estimate=COST_STACK,
        name="stack_rows",
    )(ids, shifts, got_o, got_e, fine)


def window_kernel(last, count, ids, shifts, left, mid, right, q, gain, w_k, w_v, *refs):
    weights, (out, lse), held = refs[:count], refs[count : count + 2], refs[count + 2 : 2 * count + 2]
    k_buf, v_buf, sems = refs[2 * count + 2 :]
    loads = [pltpu.make_async_copy(w_k, k_buf, sems.at[0]), pltpu.make_async_copy(w_v, v_buf, sems.at[1])]
    for copy in loads:
        copy.start()
    early = [
        pltpu.make_async_copy(w.at[0 : h.shape[0], 0 : h.shape[1]], h, sems.at[2 + i])
        for i, (w, h) in enumerate(zip(weights, held))
    ]
    span, width = left.shape
    strip, member = ids[0], ids[1]
    shift_row, shift_col = shifts[0], shifts[1]
    turn = lambda ref: pltpu.roll(ref[...].astype(F32).reshape(span // WS, WS, width), WS - shift_col, 1)
    a, b, c = turn(left), turn(mid), turn(right)
    stays = iota((1, WS, width), 1) < WS - shift_col
    fine = jnp.concatenate([jnp.where(stays, a, b), jnp.where(stays, b, c)], axis=0).reshape(2 * span, width)
    normed = rms(fine, gain[...]).astype(BF16)
    loads[0].wait()
    keys = jnp.dot(normed, k_buf[...], preferred_element_type=F32).astype(BF16)
    loads[1].wait()
    for copy in early:
        copy.start()
    values = jnp.dot(normed, v_buf[...], preferred_element_type=F32).astype(BF16)
    per = 2 * WS * WS
    shape = (128, 2 * per)
    query = lax.rem(iota(shape, 0), 64)
    column_q = lax.rem(query, WS)
    key = iota(shape, 1)
    block = lax.shift_right_arithmetic(key, 7)
    within = lax.bitwise_and(key, per - 1)
    column_k = block * WS - WS + shift_col + lax.bitwise_and(within, WS - 1)
    same_col = (column_q >= shift_col) == (block == 1)
    wrap_col = ((column_k < 0) & (member == 0)) | ((column_k >= WS) & (member == last[1]))
    low = iota((64, 128), 1) < HD
    lane = iota((64, 128), 1)
    own = (iota((128, 128), 0) < 64) == (iota((128, 128), 1) < HD)
    for half in range(2):
        row_q = WS * half + lax.shift_right_arithmetic(query, 3)
        line_k = WS * half + lax.shift_right_arithmetic(within, 3)
        row_k = line_k + shift_row - WS
        same_row = lax.shift_right_arithmetic(row_q - shift_row + WS, 3) == lax.shift_right_arithmetic(line_k, 3)
        wrap_row = ((row_k < 0) & (strip == 0)) | ((row_k >= 2 * WS) & (strip == last[0]))
        seen = same_row & same_col & jnp.logical_not(wrap_row | wrap_col)
        rows = slice(64 * half, 64 * half + 64)
        pick = lambda x: jnp.concatenate(
            [x[span * i + 64 * half : span * i + 64 * half + per] for i in range(2)], axis=0
        )
        keys_h, values_h = pick(keys), pick(values)
        marks = jnp.zeros((64, 128), F32)
        for pair in range(HEADS // 2):
            lanes = slice(128 * pair, 128 * pair + 128)
            q_pair = q[rows, lanes]
            q_both = jnp.concatenate([q_pair, q_pair], axis=0)
            q_both = jnp.where(own, q_both, jnp.zeros_like(q_both))
            score = lax.dot_general(
                q_both, keys_h[:, lanes], (((1,), (1,)), ((), ())), preferred_element_type=F32
            )
            score = jnp.where(seen, score, LOW)
            peak = jnp.max(score, axis=-1, keepdims=True)
            weight = jnp.exp(score - peak)
            total = jnp.sum(weight, axis=-1, keepdims=True)
            mixed = jnp.dot(weight.astype(BF16), values_h[:, lanes], preferred_element_type=F32) / total
            out[rows, lanes] = jnp.where(low, mixed[:64], mixed[64:])
            level = peak + jnp.log(total)
            marks = jnp.where(lane == 2 * pair, level[:64], marks)
            marks = jnp.where(lane == 2 * pair + 1, level[64:], marks)
        lse[rows, :] = marks
    for copy in early:
        copy.wait()


def window_attention(ids, shifts, left, mid, right, q, gain, w_k, w_v, weights, last):
    n_tok, width = q.shape
    count = len(weights)
    vmem = pl.BlockSpec(memory_space=pltpu.VMEM)
    smem = pl.BlockSpec(memory_space=pltpu.SMEM)
    return pl.pallas_call(
        lambda *refs: window_kernel(last, count, *refs),
        in_specs=[smem, smem] + [vmem] * 5 + [pl.BlockSpec(memory_space=pltpu.HBM)] * (2 + count),
        out_specs=[vmem] * (2 + count),
        out_shape=[
            jax.ShapeDtypeStruct((n_tok, width), F32),
            jax.ShapeDtypeStruct((n_tok, 128), F32),
        ]
        + [jax.ShapeDtypeStruct((min(w.shape[0], CHUNK), min(w.shape[1], CHUNK)), w.dtype) for w in weights],
        scratch_shapes=[
            pltpu.VMEM((width, width), BF16),
            pltpu.VMEM((width, width), BF16),
            pltpu.SemaphoreType.DMA((2 + count,)),
        ],
        compiler_params=pltpu.CompilerParams(vmem_limit_bytes=VMEM_LIMIT),
        cost_estimate=COST,
        name="window_attention",
    )(ids, shifts, left, mid, right, q, gain, w_k, w_v, *weights)


def attend(q, kv, kv_t):
    score = jnp.dot(kv, jnp.concatenate([q, jnp.zeros_like(q)], axis=0), preferred_element_type=F32)
    peak = jnp.max(score, axis=0, keepdims=True)
    weight = jnp.exp(score - peak)
    sums = jnp.sum(weight, axis=0, keepdims=True)
    mixed = jnp.dot(kv_t, weight.astype(BF16), preferred_element_type=F32)
    level = peak + jnp.log(sums)
    first = level.astype(BF16).astype(F32)
    second = (level - first).astype(BF16).astype(F32)
    third = level - first - second
    line = iota((16, q.shape[1]), 0)
    marks = jnp.where(line == 0, first, jnp.where(line == 1, second, jnp.where(line == 2, third, 0.0)))
    return jnp.concatenate([mixed[HD:] / sums, marks], axis=0)


def swap_halves(x):
    return pltpu.roll(x, 64, 1)


def top_rows(q_t, group):
    low = iota((1, 128), 1) < 64
    tiles = []
    for pair in range(2):
        a, b = (q_t[4 * group + 2 * pair + k].astype(F32) for k in range(2))
        tiles.append(jnp.where(low, a, swap_halves(b)).astype(BF16))
    return jnp.concatenate(tiles, axis=1)


def bottom_rows(q_t, group):
    low = iota((1, 128), 1) < 64
    tiles = []
    for pair in range(2):
        a, b = (q_t[4 * group + 2 * pair + k].astype(F32) for k in range(2))
        tiles.append(jnp.where(low, swap_halves(a), b).astype(BF16))
    return jnp.concatenate(tiles, axis=1)


def here_kernel(total, ids, table, q_t, own, got_o, got_e, out, store, turned):
    n_own = own.shape[0]
    per_strip = n_own // 128
    even = lax.rem(ids[0], 2) == 0
    blocked = lambda ref: ref[0:n_own, :].reshape(per_strip, 128, 128)
    above, below = blocked(got_o), blocked(got_e)
    store[0:per_strip] = jnp.where(even, above, below)
    store[per_strip : 2 * per_strip] = blocked(own)
    store[2 * per_strip :] = jnp.where(even, below, above)
    chosen = local_blocks(ids, table, per_strip, total)
    kv = jnp.concatenate([store[b] for b in chosen], axis=0)
    turned[...] = kv.astype(F32).T.astype(BF16)
    kv_t = turned[...]
    low = iota((1, 128), 1) < 64
    for group in range(q_t.shape[0] // 4):
        top = attend(top_rows(q_t, group), kv, kv_t)
        bottom = attend(bottom_rows(q_t, group), kv, kv_t)
        for pair in range(2):
            lanes = slice(128 * pair, 128 * pair + 128)
            t, u = top[:, lanes], bottom[:, lanes]
            out[4 * group + 2 * pair] = jnp.where(low, t, swap_halves(u)).astype(BF16)
            out[4 * group + 2 * pair + 1] = jnp.where(low, swap_halves(t), u).astype(BF16)


def here_attention(ids, table, q_t, own, got_o, got_e, total):
    vmem = pl.BlockSpec(memory_space=pltpu.VMEM)
    smem = pl.BlockSpec(memory_space=pltpu.SMEM)
    members, _, n_tok = q_t.shape
    return pl.pallas_call(
        lambda *refs: here_kernel(total, *refs),
        in_specs=[smem, smem] + [vmem] * 4,
        out_specs=vmem,
        out_shape=jax.ShapeDtypeStruct((members, HD + 16, n_tok), BF16),
        scratch_shapes=[
            pltpu.VMEM((3 * own.shape[0] // 128, 128, 128), BF16),
            pltpu.VMEM((128, 128 * table.shape[1]), BF16),
        ],
        compiler_params=pltpu.CompilerParams(vmem_limit_bytes=VMEM_LIMIT),
        cost_estimate=COST_HERE,
        name="here_attention",
    )(ids, table, q_t, own, got_o, got_e)


def choose_kernel(after, ids, table, far_straight, far_handed, got_o, got_e, own, kv, kv_t, store):
    n_own = own.shape[0]
    per_strip = n_own // 128
    even = lax.rem(ids[0], 2) == 0
    blocked = lambda ref: ref[0:n_own, :].reshape(per_strip, 128, 128)
    handed = lax.rem(ids[0], PLANE) == 1
    store[0:per_strip] = jnp.where(handed, blocked(far_handed), blocked(far_straight))
    store[per_strip : 2 * per_strip] = jnp.where(even, blocked(got_o), blocked(got_e))
    store[2 * per_strip :] = blocked(own)
    for i in range(table.shape[0]):
        block = store[table[i]]
        at = slice(128 * i, 128 * i + 128)
        kv[at, :] = block
        kv_t[:, at] = block.astype(F32).T.astype(BF16)


def choose_blocks(after, ids, table, far_straight, far_handed, got_o, got_e, own):
    vmem = pl.BlockSpec(memory_space=pltpu.VMEM)
    smem = pl.BlockSpec(memory_space=pltpu.SMEM)
    keys = 128 * table.shape[0]
    return pl.pallas_call(
        choose_kernel,
        in_specs=[pl.BlockSpec(memory_space=pl.ANY), smem, smem] + [vmem] * 5,
        out_specs=[vmem] * 2,
        out_shape=[jax.ShapeDtypeStruct((keys, 128), BF16), jax.ShapeDtypeStruct((128, keys), BF16)],
        scratch_shapes=[pltpu.VMEM((3 * own.shape[0] // 128, 128, 128), BF16)],
        compiler_params=pltpu.CompilerParams(vmem_limit_bytes=VMEM_LIMIT),
        cost_estimate=COST_CHOOSE,
        name="choose_blocks",
    )(after, ids, table, far_straight, far_handed, got_o, got_e, own)


def before_kernel(after, after_too, shifts, q_t, kv, kv_t, here, out):
    lane = iota((1, 128), 1)
    earlier = lane < WS * shifts[0]
    for group in range(q_t.shape[0] // 4):
        top = attend(top_rows(q_t, group), kv[...], kv_t[...])
        for pair in range(2):
            t = top[:, 128 * pair : 128 * pair + 128]
            for k in range(2):
                m = 4 * group + 2 * pair + k
                mine = t if k == 0 else swap_halves(t)
                out[m] = jnp.where(earlier, mine, here[m].astype(F32)).astype(BF16)


def before_attention(after, after_too, shifts, q_t, kv, kv_t, here):
    vmem = pl.BlockSpec(memory_space=pltpu.VMEM)
    return pl.pallas_call(
        before_kernel,
        in_specs=[pl.BlockSpec(memory_space=pl.ANY)] * 2 + [pl.BlockSpec(memory_space=pltpu.SMEM)] + [vmem] * 4,
        out_specs=vmem,
        out_shape=jax.ShapeDtypeStruct(here.shape, BF16),
        compiler_params=pltpu.CompilerParams(vmem_limit_bytes=VMEM_LIMIT),
        cost_estimate=COST,
        name="before_attention",
    )(after, after_too, shifts, q_t, kv, kv_t, here)


def finish_kernel(
    fine, near, near_lse, coarse, gain, w_out, gate_0, up_0, down_0, w_gate, w_up, w_down, out, g_buf, u_buf, d_buf, sems
):
    steps = w_gate.shape[1] // CHUNK
    loads = []
    for i in range(1, steps):
        at = pl.ds(CHUNK * i, CHUNK)
        loads.append(
            [
                pltpu.make_async_copy(w_gate.at[:, at], g_buf.at[i - 1], sems.at[3 * i - 3]),
                pltpu.make_async_copy(w_up.at[:, at], u_buf.at[i - 1], sems.at[3 * i - 2]),
                pltpu.make_async_copy(w_down.at[at], d_buf.at[i - 1], sems.at[3 * i - 1]),
            ]
        )
    for group in loads:
        for copy in group:
            copy.start()
    heads = coarse.shape[0]
    far = jnp.concatenate([coarse[h, 0:HD, :].astype(F32) for h in range(heads)], axis=0).T
    marks = [coarse[h, HD : HD + 16, :].astype(F32) for h in range(heads)]
    level = jnp.concatenate([m[0:1] + m[1:2] + m[2:3] for m in marks], axis=0).T
    diff = near_lse[:, 0:heads] - level
    share = 1.0 / (1.0 + jnp.exp(diff))
    share = jnp.concatenate(
        [jnp.broadcast_to(share[:, h : h + 1], (share.shape[0], HD)) for h in range(heads)], axis=1
    )
    head_out = (near[...] * (1.0 - share) + far * share).astype(BF16)
    mid = fine[...].astype(F32) + jnp.dot(head_out, w_out[...], preferred_element_type=F32)
    normed = rms(mid, gain[...]).astype(BF16)
    total = mid
    for i in range(steps):
        if i == 0:
            parts = (gate_0, up_0, down_0)
        else:
            for copy in loads[i - 1]:
                copy.wait()
            parts = (g_buf.at[i - 1], u_buf.at[i - 1], d_buf.at[i - 1])
        gate = jnp.dot(normed, parts[0][...], preferred_element_type=F32)
        up = jnp.dot(normed, parts[1][...], preferred_element_type=F32)
        hidden = (gate * (1.0 / (1.0 + jnp.exp(-gate))) * up).astype(BF16)
        total = total + jnp.dot(hidden, parts[2][...], preferred_element_type=F32)
    out[...] = total.astype(BF16)


def finish(fine, near, near_lse, coarse, gain, w_out, gate_0, up_0, down_0, w_gate, w_up, w_down):
    n_tok, width = fine.shape
    rest = w_gate.shape[1] // CHUNK - 1
    vmem = pl.BlockSpec(memory_space=pltpu.VMEM)
    hbm = pl.BlockSpec(memory_space=pltpu.HBM)
    return pl.pallas_call(
        finish_kernel,
        in_specs=[vmem] * 9 + [hbm] * 3,
        out_specs=vmem,
        out_shape=jax.ShapeDtypeStruct((n_tok, width), BF16),
        scratch_shapes=[
            pltpu.VMEM((rest, width, CHUNK), BF16),
            pltpu.VMEM((rest, width, CHUNK), BF16),
            pltpu.VMEM((rest, CHUNK, width), BF16),
            pltpu.SemaphoreType.DMA((3 * rest,)),
        ],
        compiler_params=pltpu.CompilerParams(vmem_limit_bytes=VMEM_LIMIT),
        cost_estimate=COST,
        name="finish",
    )(fine, near, near_lse, coarse, gain, w_out, gate_0, up_0, down_0, w_gate, w_up, w_down)


def local(
    fine,
    coarse,
    block_table,
    shifts,
    attn_gain,
    w_query,
    w_key,
    w_value,
    w_out,
    coarse_key,
    coarse_value,
    mlp_gain,
    w_gate,
    w_up,
    w_down,
):
    strips = lax.axis_size("tile")
    members = lax.axis_size("narrow")
    strip = lax.axis_index("tile").astype(jnp.int32)
    member = lax.axis_index("narrow").astype(jnp.int32)
    ids = jnp.stack([strip, member])
    rows, columns, width = fine.shape
    blocks, block_tokens, cw = coarse.shape
    total = blocks * strips
    n_own = blocks * block_tokens
    flat = fine.reshape(rows * columns, width)
    table = block_table
    gain = attn_gain.reshape(1, width)

    stay = lambda x: pltpu.with_memory_space_constraint(x, pltpu.HBM)
    flat_hbm = stay(flat)
    kv, pay_o, pay_e = project(
        ids, stay(table), stay(coarse.reshape(n_own, cw)), stay(coarse_key), stay(coarse_value), flat_hbm, total
    )
    odd_pairs = [(i, (i - 1) % strips if i % 2 == 0 else (i + 1) % strips) for i in range(strips)]
    even_pairs = [(i, i ^ 1) for i in range(strips)]
    got_o = lax.ppermute(pay_o, "tile", odd_pairs)
    got_e = lax.ppermute(pay_e, "tile", even_pairs)
    far_straight = lax.ppermute(
        kv, "tile", [(i, (i + 2) % strips) for i in range(strips) if i % PLANE != PLANE - 1]
    )
    q, q_t = queries(kv, flat_hbm, gain, stay(w_query))
    q_head = lax.all_to_all(q_t, "narrow", 0, 0, tiled=True)

    far_handed = lax.ppermute(got_o, "tile", [(i, i + 1) for i in range(0, strips, PLANE)])
    mark_row = n_own + HALO * WS * (width // 128)
    table_before = jnp.where(strip % 2 == 0, got_o[mark_row, :8], got_e[mark_row, :8]).astype(jnp.int32)

    stacked = stack_rows(ids, shifts, got_o, got_e, flat, n_own)
    stacked, table_before = lax.optimization_barrier((stacked, table_before))
    right_of = lax.ppermute(stacked, "narrow", [(i, i - 1) for i in range(1, members)])
    left_of = lax.ppermute(stacked, "narrow", [(i, i + 1) for i in range(members - 1)])
    here = here_attention(ids, table, q_head, kv, got_o, got_e, total)
    kv_before, kv_before_t = choose_blocks(here, ids, table_before, far_straight, far_handed, got_o, got_e, kv)
    from_coarse = before_attention(left_of, right_of, shifts, q_head, kv_before, kv_before_t, here)
    from_coarse = lax.all_to_all(from_coarse, "narrow", 0, 0, tiled=True)
    near, near_lse, *held = window_attention(
        ids,
        shifts,
        left_of,
        stacked,
        right_of,
        q,
        gain,
        stay(w_key),
        stay(w_value),
        (stay(w_out), stay(w_gate), stay(w_up), stay(w_down)),
        (strips - 1, members - 1),
    )
    out = finish(
        flat,
        near,
        near_lse,
        from_coarse,
        mlp_gain.reshape(1, width),
        *held,
        stay(w_gate),
        stay(w_up),
        stay(w_down),
    )
    return out.reshape(rows, columns, width)


def solution(mesh):
    placed = (
        P("tile", "narrow", None),
        P("tile", None, None),
        P("tile", None),
    ) + (P(),) * 12
    return jax.shard_map(
        local, mesh=mesh, in_specs=placed, out_specs=P("tile", "narrow", None), check_vma=False
    )
```

```python
import jax
import jax.numpy as jnp
from jax import lax
from jax.experimental import pallas as pl
from jax.experimental.pallas import tpu as pltpu
from jax.sharding import PartitionSpec as P

HEADS = 8
HD = 64
WS = 8
HALO = WS - 1
PLANE = 16
CHUNK = 512
EPS = 1e-06
F32 = jnp.float32
BF16 = jnp.bfloat16
LOW = -1e30
VMEM_LIMIT = 24 * 1024 * 1024
COST = pl.CostEstimate(flops=1000, bytes_accessed=1000, transcendentals=0)
COST_STACK = pl.CostEstimate(flops=10000000000, bytes_accessed=1000, transcendentals=0)
COST_HERE = pl.CostEstimate(flops=1000, bytes_accessed=1000, transcendentals=0)
COST_CHOOSE = pl.CostEstimate(flops=10000000000, bytes_accessed=1000, transcendentals=0)


def iota(shape, dim):
    return lax.broadcasted_iota(jnp.int32, shape, dim)


def rms(x, gain):
    mean_square = jnp.mean(x * x, axis=-1, keepdims=True)
    return x * lax.rsqrt(mean_square + EPS) * gain


def local_blocks(ids, table, per_strip, total):
    first = (ids[0] - 1) * per_strip
    return [lax.rem(table[0, i] - first + 2 * total, total) for i in range(table.shape[1])]


def edge_rows(x, top):
    n_tok, width = x.shape
    halo = HALO * WS
    parts = []
    for c in range(width // 128):
        lanes = slice(128 * c, 128 * c + 128)
        first, last = x[0:64, lanes].astype(F32), x[n_tok - 64 :, lanes].astype(F32)
        parts.append(jnp.where(top, first[0:halo], last[64 - halo :]))
    return jnp.concatenate(parts, axis=0).astype(BF16)


def project_kernel(total, ids, table_in, coarse, w_k, w_v, fine, kv, pay_o, pay_e, table, c_buf, w_buf, x_buf, sems):
    chunks = c_buf.shape[0]
    rows = c_buf.shape[1]
    cols = pl.ds(pl.multiple_of(ids[1] // 2 * 128, 128), 128)
    loads = [
        pltpu.make_async_copy(w_k.at[:, cols], w_buf.at[:, 0:128], sems.at[0]),
        pltpu.make_async_copy(w_v.at[:, cols], w_buf.at[:, 128:256], sems.at[1]),
        pltpu.make_async_copy(fine, x_buf, sems.at[2]),
        pltpu.make_async_copy(table_in, table, sems.at[3 + chunks]),
    ]
    parts = [
        pltpu.make_async_copy(coarse.at[pl.ds(rows * i, rows)], c_buf.at[i], sems.at[3 + i])
        for i in range(chunks)
    ]
    for copy in (loads[0], loads[1], *parts, loads[2], loads[3]):
        copy.start()
    odd_head = lax.rem(ids[1], 2) == 1
    even = lax.rem(ids[0], 2) == 0
    low = iota((rows, 128), 1) < HD
    base = kv.shape[0]
    n_tok, width = x_buf.shape
    half = n_tok // 2
    loads[0].wait()
    loads[1].wait()
    for i in range(chunks):
        parts[i].wait()
        tokens = c_buf[i]
        product = jnp.dot(tokens, w_buf[...], preferred_element_type=F32)
        key, value = product[:, 0:128], product[:, 128:256]
        key = jnp.where(odd_head, pltpu.roll(key, HD, 1), key)
        value = jnp.where(odd_head, value, pltpu.roll(value, HD, 1))
        both = jnp.where(low, key, value).astype(BF16)
        at = slice(rows * i, rows * i + rows)
        kv[at, :] = both
        pay_o[at, :] = both
        pay_e[at, :] = both
    loads[3].wait()
    chosen = local_blocks(ids, table, base // 128, total)
    lane = iota((16, 128), 1)
    marks = jnp.zeros((16, 128), F32)
    for i, b in enumerate(chosen):
        marks = jnp.where(lane == i, b.astype(F32), marks)
    end = base + HALO * WS * (width // 128)
    pay_o[end : end + 16, :] = marks.astype(BF16)
    pay_e[end : end + 16, :] = marks.astype(BF16)
    loads[2].wait()
    pay_o[base:end, :] = edge_rows(x_buf, even)
    pay_e[base:end, :] = edge_rows(x_buf, jnp.logical_not(even))


def project(ids, table, coarse, w_k, w_v, fine, total):
    n_coarse, cw = coarse.shape
    n_tok, width = fine.shape
    chunks = 1
    pay_rows = n_coarse + HALO * WS * (width // 128) + 16
    smem = pl.BlockSpec(memory_space=pltpu.SMEM)
    hbm = pl.BlockSpec(memory_space=pltpu.HBM)
    vmem = pl.BlockSpec(memory_space=pltpu.VMEM)
    return pl.pallas_call(
        lambda *refs: project_kernel(total, *refs),
        in_specs=[smem] + [hbm] * 5,
        out_specs=[vmem] * 3,
        out_shape=[
            jax.ShapeDtypeStruct((n_coarse, 128), BF16),
            jax.ShapeDtypeStruct((pay_rows, 128), BF16),
            jax.ShapeDtypeStruct((pay_rows, 128), BF16),
        ],
        scratch_shapes=[
            pltpu.SMEM(table.shape, jnp.int32),
            pltpu.VMEM((chunks, n_coarse // chunks, cw), BF16),
            pltpu.VMEM((cw, 256), BF16),
            pltpu.VMEM((n_tok, width), BF16),
            pltpu.SemaphoreType.DMA((4 + chunks,)),
        ],
        compiler_params=pltpu.CompilerParams(vmem_limit_bytes=VMEM_LIMIT),
        cost_estimate=COST,
        name="project",
    )(ids, table, coarse, w_k, w_v, fine)


def query_kernel(after, fine, gain, w_q, q_nat, q_t, x_buf, q_buf, sems):
    first = pltpu.make_async_copy(fine, x_buf, sems.at[0])
    second = pltpu.make_async_copy(w_q, q_buf, sems.at[1])
    first.start()
    second.start()
    first.wait()
    normed = rms(x_buf[...].astype(F32), gain[...]).astype(BF16)
    second.wait()
    q = jnp.dot(normed, q_buf[...], preferred_element_type=F32) * (1.0 / HD**0.5)
    q_nat[...] = q.astype(BF16)
    q_t[...] = q.T.astype(BF16).reshape(q_t.shape)


def queries(after, fine, gain, w_q):
    n_tok, width = fine.shape
    hbm = pl.BlockSpec(memory_space=pltpu.HBM)
    vmem = pl.BlockSpec(memory_space=pltpu.VMEM)
    return pl.pallas_call(
        query_kernel,
        in_specs=[pl.BlockSpec(memory_space=pl.ANY), hbm, vmem, hbm],
        out_specs=[vmem] * 2,
        out_shape=[
            jax.ShapeDtypeStruct((n_tok, width), BF16),
            jax.ShapeDtypeStruct((HEADS, HD, n_tok), BF16),
        ],
        scratch_shapes=[
            pltpu.VMEM((n_tok, width), BF16),
            pltpu.VMEM((width, width), BF16),
            pltpu.SemaphoreType.DMA((2,)),
        ],
        compiler_params=pltpu.CompilerParams(vmem_limit_bytes=VMEM_LIMIT),
        cost_estimate=COST,
        name="queries",
    )(after, fine, gain, w_q)


def stack_kernel(ids, shifts, base, got_o, got_e, fine, out, rows):
    n_tok, width = fine.shape
    half = n_tok // 2
    even = lax.rem(ids[0], 2) == 0
    rows[half : half + n_tok, :] = fine[...].astype(F32)
    halo = HALO * WS
    end = base + halo * (width // 128)
    a, b = got_o[base:end, :].astype(F32), got_e[base:end, :].astype(F32)
    above, below = jnp.where(even, a, b), jnp.where(even, b, a)
    for c in range(width // 128):
        lanes = slice(128 * c, 128 * c + 128)
        at = slice(halo * c, halo * c + halo)
        rows[half - halo : half, lanes] = above[at]
        rows[half + n_tok : half + n_tok + halo, lanes] = below[at]
    out[...] = rows[pl.ds(pl.multiple_of(shifts[0] * WS, WS), out.shape[0]), :].astype(BF16)


def stack_rows(ids, shifts, got_o, got_e, fine, base):
    n_tok, width = fine.shape
    vmem = pl.BlockSpec(memory_space=pltpu.VMEM)
    smem = pl.BlockSpec(memory_space=pltpu.SMEM)
    return pl.pallas_call(
        lambda ids, shifts, *refs: stack_kernel(ids, shifts, base, *refs),
        in_specs=[smem, smem] + [vmem] * 3,
        out_specs=vmem,
        out_shape=jax.ShapeDtypeStruct((n_tok + n_tok // 2, width), BF16),
        scratch_shapes=[pltpu.VMEM((2 * n_tok, width), F32)],
        compiler_params=pltpu.CompilerParams(vmem_limit_bytes=VMEM_LIMIT),
        cost_estimate=COST_STACK,
        name="stack_rows",
    )(ids, shifts, got_o, got_e, fine)


def window_kernel(last, count, ids, shifts, left, mid, right, q, gain, w_k, w_v, *refs):
    weights, (out, lse), held = refs[:count], refs[count : count + 2], refs[count + 2 : 2 * count + 2]
    k_buf, v_buf, sems = refs[2 * count + 2 :]
    loads = [pltpu.make_async_copy(w_k, k_buf, sems.at[0]), pltpu.make_async_copy(w_v, v_buf, sems.at[1])]
    for copy in loads:
        copy.start()
    early = [
        pltpu.make_async_copy(w.at[0 : h.shape[0], 0 : h.shape[1]], h, sems.at[2 + i])
        for i, (w, h) in enumerate(zip(weights, held))
    ]
    span, width = left.shape
    strip, member = ids[0], ids[1]
    shift_row, shift_col = shifts[0], shifts[1]
    turn = lambda ref: pltpu.roll(ref[...].astype(F32).reshape(span // WS, WS, width), WS - shift_col, 1)
    a, b, c = turn(left), turn(mid), turn(right)
    stays = iota((1, WS, width), 1) < WS - shift_col
    fine = jnp.concatenate([jnp.where(stays, a, b), jnp.where(stays, b, c)], axis=0).reshape(2 * span, width)
    normed = rms(fine, gain[...]).astype(BF16)
    loads[0].wait()
    keys = jnp.dot(normed, k_buf[...], preferred_element_type=F32).astype(BF16)
    loads[1].wait()
    for copy in early:
        copy.start()
    values = jnp.dot(normed, v_buf[...], preferred_element_type=F32).astype(BF16)
    per = 2 * WS * WS
    shape = (128, 2 * per)
    query = lax.rem(iota(shape, 0), 64)
    column_q = lax.rem(query, WS)
    key = iota(shape, 1)
    block = lax.shift_right_arithmetic(key, 7)
    within = lax.bitwise_and(key, per - 1)
    column_k = block * WS - WS + shift_col + lax.bitwise_and(within, WS - 1)
    same_col = (column_q >= shift_col) == (block == 1)
    wrap_col = ((column_k < 0) & (member == 0)) | ((column_k >= WS) & (member == last[1]))
    low = iota((64, 128), 1) < HD
    lane = iota((64, 128), 1)
    own = (iota((128, 128), 0) < 64) == (iota((128, 128), 1) < HD)
    for half in range(2):
        row_q = WS * half + lax.shift_right_arithmetic(query, 3)
        line_k = WS * half + lax.shift_right_arithmetic(within, 3)
        row_k = line_k + shift_row - WS
        same_row = lax.shift_right_arithmetic(row_q - shift_row + WS, 3) == lax.shift_right_arithmetic(line_k, 3)
        wrap_row = ((row_k < 0) & (strip == 0)) | ((row_k >= 2 * WS) & (strip == last[0]))
        seen = same_row & same_col & jnp.logical_not(wrap_row | wrap_col)
        rows = slice(64 * half, 64 * half + 64)
        pick = lambda x: jnp.concatenate(
            [x[span * i + 64 * half : span * i + 64 * half + per] for i in range(2)], axis=0
        )
        keys_h, values_h = pick(keys), pick(values)
        marks = jnp.zeros((64, 128), F32)
        for pair in range(HEADS // 2):
            lanes = slice(128 * pair, 128 * pair + 128)
            q_pair = q[rows, lanes]
            q_both = jnp.concatenate([q_pair, q_pair], axis=0)
            q_both = jnp.where(own, q_both, jnp.zeros_like(q_both))
            score = lax.dot_general(
                q_both, keys_h[:, lanes], (((1,), (1,)), ((), ())), preferred_element_type=F32
            )
            score = jnp.where(seen, score, LOW)
            peak = jnp.max(score, axis=-1, keepdims=True)
            weight = jnp.exp(score - peak)
            total = jnp.sum(weight, axis=-1, keepdims=True)
            mixed = jnp.dot(weight.astype(BF16), values_h[:, lanes], preferred_element_type=F32) / total
            out[rows, lanes] = jnp.where(low, mixed[:64], mixed[64:])
            level = peak + jnp.log(total)
            marks = jnp.where(lane == 2 * pair, level[:64], marks)
            marks = jnp.where(lane == 2 * pair + 1, level[64:], marks)
        lse[rows, :] = marks
    for copy in early:
        copy.wait()


def window_attention(ids, shifts, left, mid, right, q, gain, w_k, w_v, weights, last):
    n_tok, width = q.shape
    count = len(weights)
    vmem = pl.BlockSpec(memory_space=pltpu.VMEM)
    smem = pl.BlockSpec(memory_space=pltpu.SMEM)
    return pl.pallas_call(
        lambda *refs: window_kernel(last, count, *refs),
        in_specs=[smem, smem] + [vmem] * 5 + [pl.BlockSpec(memory_space=pltpu.HBM)] * (2 + count),
        out_specs=[vmem] * (2 + count),
        out_shape=[
            jax.ShapeDtypeStruct((n_tok, width), F32),
            jax.ShapeDtypeStruct((n_tok, 128), F32),
        ]
        + [jax.ShapeDtypeStruct((min(w.shape[0], CHUNK), min(w.shape[1], CHUNK)), w.dtype) for w in weights],
        scratch_shapes=[
            pltpu.VMEM((width, width), BF16),
            pltpu.VMEM((width, width), BF16),
            pltpu.SemaphoreType.DMA((2 + count,)),
        ],
        compiler_params=pltpu.CompilerParams(vmem_limit_bytes=VMEM_LIMIT),
        cost_estimate=COST,
        name="window_attention",
    )(ids, shifts, left, mid, right, q, gain, w_k, w_v, *weights)


def attend(q, kv, kv_t):
    score = jnp.dot(kv, jnp.concatenate([q, jnp.zeros_like(q)], axis=0), preferred_element_type=F32)
    peak = jnp.max(score, axis=0, keepdims=True)
    weight = jnp.exp(score - peak)
    sums = jnp.sum(weight, axis=0, keepdims=True)
    mixed = jnp.dot(kv_t, weight.astype(BF16), preferred_element_type=F32)
    level = peak + jnp.log(sums)
    first = level.astype(BF16).astype(F32)
    second = (level - first).astype(BF16).astype(F32)
    third = level - first - second
    line = iota((16, q.shape[1]), 0)
    marks = jnp.where(line == 0, first, jnp.where(line == 1, second, jnp.where(line == 2, third, 0.0)))
    return jnp.concatenate([mixed[HD:] / sums, marks], axis=0)


def swap_halves(x):
    return pltpu.roll(x, 64, 1)


def top_rows(q_t, group):
    low = iota((1, 128), 1) < 64
    tiles = []
    for pair in range(4):
        a, b = (q_t[8 * group + 2 * pair + k].astype(F32) for k in range(2))
        tiles.append(jnp.where(low, a, swap_halves(b)).astype(BF16))
    return jnp.concatenate(tiles, axis=1)


def bottom_rows(q_t, group):
    low = iota((1, 128), 1) < 64
    tiles = []
    for pair in range(4):
        a, b = (q_t[8 * group + 2 * pair + k].astype(F32) for k in range(2))
        tiles.append(jnp.where(low, swap_halves(a), b).astype(BF16))
    return jnp.concatenate(tiles, axis=1)


def here_kernel(total, ids, table, q_t, own, got_o, got_e, out, store, turned):
    n_own = own.shape[0]
    per_strip = n_own // 128
    even = lax.rem(ids[0], 2) == 0
    blocked = lambda ref: ref[0:n_own, :].reshape(per_strip, 128, 128)
    above, below = blocked(got_o), blocked(got_e)
    store[0:per_strip] = jnp.where(even, above, below)
    store[per_strip : 2 * per_strip] = blocked(own)
    store[2 * per_strip :] = jnp.where(even, below, above)
    chosen = local_blocks(ids, table, per_strip, total)
    kv = jnp.concatenate([store[b] for b in chosen], axis=0)
    turned[...] = kv.astype(F32).T.astype(BF16)
    kv_t = turned[...]
    low = iota((1, 128), 1) < 64
    for group in range(q_t.shape[0] // 8):
        top = attend(top_rows(q_t, group), kv, kv_t)
        bottom = attend(bottom_rows(q_t, group), kv, kv_t)
        for pair in range(4):
            lanes = slice(128 * pair, 128 * pair + 128)
            t, u = top[:, lanes], bottom[:, lanes]
            out[8 * group + 2 * pair] = jnp.where(low, t, swap_halves(u)).astype(BF16)
            out[8 * group + 2 * pair + 1] = jnp.where(low, swap_halves(t), u).astype(BF16)


def here_attention(ids, table, q_t, own, got_o, got_e, total):
    vmem = pl.BlockSpec(memory_space=pltpu.VMEM)
    smem = pl.BlockSpec(memory_space=pltpu.SMEM)
    members, _, n_tok = q_t.shape
    return pl.pallas_call(
        lambda *refs: here_kernel(total, *refs),
        in_specs=[smem, smem] + [vmem] * 4,
        out_specs=vmem,
        out_shape=jax.ShapeDtypeStruct((members, HD + 16, n_tok), BF16),
        scratch_shapes=[
            pltpu.VMEM((3 * own.shape[0] // 128, 128, 128), BF16),
            pltpu.VMEM((128, 128 * table.shape[1]), BF16),
        ],
        compiler_params=pltpu.CompilerParams(vmem_limit_bytes=VMEM_LIMIT),
        cost_estimate=COST_HERE,
        name="here_attention",
    )(ids, table, q_t, own, got_o, got_e)


def choose_kernel(after, ids, table, far_straight, far_handed, got_o, got_e, own, kv, kv_t, store):
    n_own = own.shape[0]
    per_strip = n_own // 128
    even = lax.rem(ids[0], 2) == 0
    blocked = lambda ref: ref[0:n_own, :].reshape(per_strip, 128, 128)
    handed = lax.rem(ids[0], PLANE) == 1
    store[0:per_strip] = jnp.where(handed, blocked(far_handed), blocked(far_straight))
    store[per_strip : 2 * per_strip] = jnp.where(even, blocked(got_o), blocked(got_e))
    store[2 * per_strip :] = blocked(own)
    for i in range(table.shape[0]):
        block = store[table[i]]
        at = slice(128 * i, 128 * i + 128)
        kv[at, :] = block
        kv_t[:, at] = block.astype(F32).T.astype(BF16)


def choose_blocks(after, ids, table, far_straight, far_handed, got_o, got_e, own):
    vmem = pl.BlockSpec(memory_space=pltpu.VMEM)
    smem = pl.BlockSpec(memory_space=pltpu.SMEM)
    keys = 128 * table.shape[0]
    return pl.pallas_call(
        choose_kernel,
        in_specs=[pl.BlockSpec(memory_space=pl.ANY), smem, smem] + [vmem] * 5,
        out_specs=[vmem] * 2,
        out_shape=[jax.ShapeDtypeStruct((keys, 128), BF16), jax.ShapeDtypeStruct((128, keys), BF16)],
        scratch_shapes=[pltpu.VMEM((3 * own.shape[0] // 128, 128, 128), BF16)],
        compiler_params=pltpu.CompilerParams(vmem_limit_bytes=VMEM_LIMIT),
        cost_estimate=COST_CHOOSE,
        name="choose_blocks",
    )(after, ids, table, far_straight, far_handed, got_o, got_e, own)


def before_kernel(after, after_too, shifts, q_t, kv, kv_t, here, out):
    lane = iota((1, 128), 1)
    earlier = lane < WS * shifts[0]
    for group in range(q_t.shape[0] // 8):
        top = attend(top_rows(q_t, group), kv[...], kv_t[...])
        for pair in range(4):
            t = top[:, 128 * pair : 128 * pair + 128]
            for k in range(2):
                m = 8 * group + 2 * pair + k
                mine = t if k == 0 else swap_halves(t)
                out[m] = jnp.where(earlier, mine, here[m].astype(F32)).astype(BF16)


def before_attention(after, after_too, shifts, q_t, kv, kv_t, here):
    vmem = pl.BlockSpec(memory_space=pltpu.VMEM)
    return pl.pallas_call(
        before_kernel,
        in_specs=[pl.BlockSpec(memory_space=pl.ANY)] * 2 + [pl.BlockSpec(memory_space=pltpu.SMEM)] + [vmem] * 4,
        out_specs=vmem,
        out_shape=jax.ShapeDtypeStruct(here.shape, BF16),
        compiler_params=pltpu.CompilerParams(vmem_limit_bytes=VMEM_LIMIT),
        cost_estimate=COST,
        name="before_attention",
    )(after, after_too, shifts, q_t, kv, kv_t, here)


def finish_kernel(
    fine, near, near_lse, coarse, gain, w_out, gate_0, up_0, down_0, w_gate, w_up, w_down, out, g_buf, u_buf, d_buf, sems
):
    steps = w_gate.shape[1] // CHUNK
    loads = []
    for i in range(1, steps):
        at = pl.ds(CHUNK * i, CHUNK)
        loads.append(
            [
                pltpu.make_async_copy(w_gate.at[:, at], g_buf.at[i - 1], sems.at[3 * i - 3]),
                pltpu.make_async_copy(w_up.at[:, at], u_buf.at[i - 1], sems.at[3 * i - 2]),
                pltpu.make_async_copy(w_down.at[at], d_buf.at[i - 1], sems.at[3 * i - 1]),
            ]
        )
    for group in loads:
        for copy in group:
            copy.start()
    heads = coarse.shape[0]
    far = jnp.concatenate([coarse[h, 0:HD, :].astype(F32) for h in range(heads)], axis=0).T
    marks = [coarse[h, HD : HD + 16, :].astype(F32) for h in range(heads)]
    level = jnp.concatenate([m[0:1] + m[1:2] + m[2:3] for m in marks], axis=0).T
    diff = near_lse[:, 0:heads] - level
    share = 1.0 / (1.0 + jnp.exp(diff))
    share = jnp.concatenate(
        [jnp.broadcast_to(share[:, h : h + 1], (share.shape[0], HD)) for h in range(heads)], axis=1
    )
    head_out = (near[...] * (1.0 - share) + far * share).astype(BF16)
    mid = fine[...].astype(F32) + jnp.dot(head_out, w_out[...], preferred_element_type=F32)
    normed = rms(mid, gain[...]).astype(BF16)
    total = mid
    for i in range(steps):
        if i == 0:
            parts = (gate_0, up_0, down_0)
        else:
            for copy in loads[i - 1]:
                copy.wait()
            parts = (g_buf.at[i - 1], u_buf.at[i - 1], d_buf.at[i - 1])
        gate = jnp.dot(normed, parts[0][...], preferred_element_type=F32)
        up = jnp.dot(normed, parts[1][...], preferred_element_type=F32)
        hidden = (gate * (1.0 / (1.0 + jnp.exp(-gate))) * up).astype(BF16)
        total = total + jnp.dot(hidden, parts[2][...], preferred_element_type=F32)
    out[...] = total.astype(BF16)


def finish(fine, near, near_lse, coarse, gain, w_out, gate_0, up_0, down_0, w_gate, w_up, w_down):
    n_tok, width = fine.shape
    rest = w_gate.shape[1] // CHUNK - 1
    vmem = pl.BlockSpec(memory_space=pltpu.VMEM)
    hbm = pl.BlockSpec(memory_space=pltpu.HBM)
    return pl.pallas_call(
        finish_kernel,
        in_specs=[vmem] * 9 + [hbm] * 3,
        out_specs=vmem,
        out_shape=jax.ShapeDtypeStruct((n_tok, width), BF16),
        scratch_shapes=[
            pltpu.VMEM((rest, width, CHUNK), BF16),
            pltpu.VMEM((rest, width, CHUNK), BF16),
            pltpu.VMEM((rest, CHUNK, width), BF16),
            pltpu.SemaphoreType.DMA((3 * rest,)),
        ],
        compiler_params=pltpu.CompilerParams(vmem_limit_bytes=VMEM_LIMIT),
        cost_estimate=COST,
        name="finish",
    )(fine, near, near_lse, coarse, gain, w_out, gate_0, up_0, down_0, w_gate, w_up, w_down)


def local(
    fine,
    coarse,
    block_table,
    shifts,
    attn_gain,
    w_query,
    w_key,
    w_value,
    w_out,
    coarse_key,
    coarse_value,
    mlp_gain,
    w_gate,
    w_up,
    w_down,
):
    strips = lax.axis_size("tile")
    members = lax.axis_size("narrow")
    strip = lax.axis_index("tile").astype(jnp.int32)
    member = lax.axis_index("narrow").astype(jnp.int32)
    ids = jnp.stack([strip, member])
    rows, columns, width = fine.shape
    blocks, block_tokens, cw = coarse.shape
    total = blocks * strips
    n_own = blocks * block_tokens
    flat = fine.reshape(rows * columns, width)
    table = block_table
    gain = attn_gain.reshape(1, width)

    stay = lambda x: pltpu.with_memory_space_constraint(x, pltpu.HBM)
    flat_hbm = stay(flat)
    kv, pay_o, pay_e = project(
        ids, stay(table), stay(coarse.reshape(n_own, cw)), stay(coarse_key), stay(coarse_value), flat_hbm, total
    )
    odd_pairs = [(i, (i - 1) % strips if i % 2 == 0 else (i + 1) % strips) for i in range(strips)]
    even_pairs = [(i, i ^ 1) for i in range(strips)]
    got_o = lax.ppermute(pay_o, "tile", odd_pairs)
    got_e = lax.ppermute(pay_e, "tile", even_pairs)
    far_straight = lax.ppermute(
        kv, "tile", [(i, (i + 2) % strips) for i in range(strips) if i % PLANE != PLANE - 1]
    )
    q, q_t = queries(kv, flat_hbm, gain, stay(w_query))
    q_head = lax.all_to_all(q_t, "narrow", 0, 0, tiled=True)

    far_handed = lax.ppermute(got_o, "tile", [(i, i + 1) for i in range(0, strips, PLANE)])
    mark_row = n_own + HALO * WS * (width // 128)
    table_before = jnp.where(strip % 2 == 0, got_o[mark_row, :8], got_e[mark_row, :8]).astype(jnp.int32)

    stacked = stack_rows(ids, shifts, got_o, got_e, flat, n_own)
    stacked, table_before = lax.optimization_barrier((stacked, table_before))
    right_of = lax.ppermute(stacked, "narrow", [(i, i - 1) for i in range(1, members)])
    left_of = lax.ppermute(stacked, "narrow", [(i, i + 1) for i in range(members - 1)])
    here = here_attention(ids, table, q_head, kv, got_o, got_e, total)
    kv_before, kv_before_t = choose_blocks(here, ids, table_before, far_straight, far_handed, got_o, got_e, kv)
    from_coarse = before_attention(left_of, right_of, shifts, q_head, kv_before, kv_before_t, here)
    from_coarse = lax.all_to_all(from_coarse, "narrow", 0, 0, tiled=True)
    near, near_lse, *held = window_attention(
        ids,
        shifts,
        left_of,
        stacked,
        right_of,
        q,
        gain,
        stay(w_key),
        stay(w_value),
        (stay(w_out), stay(w_gate), stay(w_up), stay(w_down)),
        (strips - 1, members - 1),
    )
    out = finish(
        flat,
        near,
        near_lse,
        from_coarse,
        mlp_gain.reshape(1, width),
        *held,
        stay(w_gate),
        stay(w_up),
        stay(w_down),
    )
    return out.reshape(rows, columns, width)


def solution(mesh):
    placed = (
        P("tile", "narrow", None),
        P("tile", None, None),
        P("tile", None),
    ) + (P(),) * 12
    return jax.shard_map(
        local, mesh=mesh, in_specs=placed, out_specs=P("tile", "narrow", None), check_vma=False
    )
```

```python
import jax
import jax.numpy as jnp
from jax import lax
from jax.experimental import pallas as pl
from jax.experimental.pallas import tpu as pltpu
from jax.sharding import PartitionSpec as P

HEADS = 8
HD = 64
WS = 8
HALO = WS - 1
PLANE = 16
CHUNK = 512
EPS = 1e-06
F32 = jnp.float32
BF16 = jnp.bfloat16
LOW = -1e30
VMEM_LIMIT = 24 * 1024 * 1024
COST = pl.CostEstimate(flops=1000, bytes_accessed=1000, transcendentals=0)
COST_STACK = pl.CostEstimate(flops=10000000000, bytes_accessed=1000, transcendentals=0)
COST_HERE = pl.CostEstimate(flops=1000, bytes_accessed=1000, transcendentals=0)
COST_CHOOSE = pl.CostEstimate(flops=10000000000, bytes_accessed=1000, transcendentals=0)


def iota(shape, dim):
    return lax.broadcasted_iota(jnp.int32, shape, dim)


def rms(x, gain):
    mean_square = jnp.mean(x * x, axis=-1, keepdims=True)
    return x * lax.rsqrt(mean_square + EPS) * gain


def local_blocks(ids, table, per_strip, total):
    first = (ids[0] - 1) * per_strip
    return [lax.rem(table[0, i] - first + 2 * total, total) for i in range(table.shape[1])]


def edge_rows(x, top):
    n_tok, width = x.shape
    halo = HALO * WS
    parts = []
    for c in range(width // 128):
        lanes = slice(128 * c, 128 * c + 128)
        first, last = x[0:64, lanes].astype(F32), x[n_tok - 64 :, lanes].astype(F32)
        parts.append(jnp.where(top, first[0:halo], last[64 - halo :]))
    return jnp.concatenate(parts, axis=0).astype(BF16)


def project_kernel(total, ids, table_in, coarse, w_k, w_v, fine, kv, pay_o, pay_e, table, c_buf, w_buf, x_buf, sems):
    chunks = c_buf.shape[0]
    rows = c_buf.shape[1]
    cols = pl.ds(pl.multiple_of(ids[1] // 2 * 128, 128), 128)
    loads = [
        pltpu.make_async_copy(w_k.at[:, cols], w_buf.at[:, 0:128], sems.at[0]),
        pltpu.make_async_copy(w_v.at[:, cols], w_buf.at[:, 128:256], sems.at[1]),
        pltpu.make_async_copy(fine, x_buf, sems.at[2]),
        pltpu.make_async_copy(table_in, table, sems.at[3 + chunks]),
    ]
    parts = [
        pltpu.make_async_copy(coarse.at[pl.ds(rows * i, rows)], c_buf.at[i], sems.at[3 + i])
        for i in range(chunks)
    ]
    for copy in (loads[0], loads[1], *parts, loads[2], loads[3]):
        copy.start()
    odd_head = lax.rem(ids[1], 2) == 1
    even = lax.rem(ids[0], 2) == 0
    low = iota((rows, 128), 1) < HD
    base = kv.shape[0]
    n_tok, width = x_buf.shape
    half = n_tok // 2
    loads[0].wait()
    loads[1].wait()
    for i in range(chunks):
        parts[i].wait()
        tokens = c_buf[i]
        product = jnp.dot(tokens, w_buf[...], preferred_element_type=F32)
        key, value = product[:, 0:128], product[:, 128:256]
        key = jnp.where(odd_head, pltpu.roll(key, HD, 1), key)
        value = jnp.where(odd_head, value, pltpu.roll(value, HD, 1))
        both = jnp.where(low, key, value).astype(BF16)
        at = slice(rows * i, rows * i + rows)
        kv[at, :] = both
        pay_o[at, :] = both
        pay_e[at, :] = both
    loads[3].wait()
    chosen = local_blocks(ids, table, base // 128, total)
    lane = iota((16, 128), 1)
    marks = jnp.zeros((16, 128), F32)
    for i, b in enumerate(chosen):
        marks = jnp.where(lane == i, b.astype(F32), marks)
    end = base + HALO * WS * (width // 128)
    pay_o[end : end + 16, :] = marks.astype(BF16)
    pay_e[end : end + 16, :] = marks.astype(BF16)
    loads[2].wait()
    pay_o[base:end, :] = edge_rows(x_buf, even)
    pay_e[base:end, :] = edge_rows(x_buf, jnp.logical_not(even))


def project(ids, table, coarse, w_k, w_v, fine, total):
    n_coarse, cw = coarse.shape
    n_tok, width = fine.shape
    chunks = 1
    pay_rows = n_coarse + HALO * WS * (width // 128) + 16
    smem = pl.BlockSpec(memory_space=pltpu.SMEM)
    hbm = pl.BlockSpec(memory_space=pltpu.HBM)
    vmem = pl.BlockSpec(memory_space=pltpu.VMEM)
    return pl.pallas_call(
        lambda *refs: project_kernel(total, *refs),
        in_specs=[smem] + [hbm] * 5,
        out_specs=[vmem] * 3,
        out_shape=[
            jax.ShapeDtypeStruct((n_coarse, 128), BF16),
            jax.ShapeDtypeStruct((pay_rows, 128), BF16),
            jax.ShapeDtypeStruct((pay_rows, 128), BF16),
        ],
        scratch_shapes=[
            pltpu.SMEM(table.shape, jnp.int32),
            pltpu.VMEM((chunks, n_coarse // chunks, cw), BF16),
            pltpu.VMEM((cw, 256), BF16),
            pltpu.VMEM((n_tok, width), BF16),
            pltpu.SemaphoreType.DMA((4 + chunks,)),
        ],
        compiler_params=pltpu.CompilerParams(vmem_limit_bytes=VMEM_LIMIT),
        cost_estimate=COST,
        name="project",
    )(ids, table, coarse, w_k, w_v, fine)


def query_kernel(after, fine, gain, w_q, q_nat, q_t, x_buf, q_buf, sems):
    first = pltpu.make_async_copy(fine, x_buf, sems.at[0])
    second = pltpu.make_async_copy(w_q, q_buf, sems.at[1])
    first.start()
    second.start()
    first.wait()
    normed = rms(x_buf[...].astype(F32), gain[...]).astype(BF16)
    second.wait()
    q = jnp.dot(normed, q_buf[...], preferred_element_type=F32) * (1.0 / HD**0.5)
    q_nat[...] = q.astype(BF16)
    q_t[...] = q.T.astype(BF16).reshape(q_t.shape)


def queries(after, fine, gain, w_q):
    n_tok, width = fine.shape
    hbm = pl.BlockSpec(memory_space=pltpu.HBM)
    vmem = pl.BlockSpec(memory_space=pltpu.VMEM)
    return pl.pallas_call(
        query_kernel,
        in_specs=[pl.BlockSpec(memory_space=pl.ANY), hbm, vmem, hbm],
        out_specs=[vmem] * 2,
        out_shape=[
            jax.ShapeDtypeStruct((n_tok, width), BF16),
            jax.ShapeDtypeStruct((HEADS, HD, n_tok), BF16),
        ],
        scratch_shapes=[
            pltpu.VMEM((n_tok, width), BF16),
            pltpu.VMEM((width, width), BF16),
            pltpu.SemaphoreType.DMA((2,)),
        ],
        compiler_params=pltpu.CompilerParams(vmem_limit_bytes=VMEM_LIMIT),
        cost_estimate=COST,
        name="queries",
    )(after, fine, gain, w_q)


def stack_kernel(ids, shifts, base, got_o, got_e, fine, out, rows):
    n_tok, width = fine.shape
    half = n_tok // 2
    even = lax.rem(ids[0], 2) == 0
    rows[half : half + n_tok, :] = fine[...].astype(F32)
    halo = HALO * WS
    end = base + halo * (width // 128)
    a, b = got_o[base:end, :].astype(F32), got_e[base:end, :].astype(F32)
    above, below = jnp.where(even, a, b), jnp.where(even, b, a)
    for c in range(width // 128):
        lanes = slice(128 * c, 128 * c + 128)
        at = slice(halo * c, halo * c + halo)
        rows[half - halo : half, lanes] = above[at]
        rows[half + n_tok : half + n_tok + halo, lanes] = below[at]
    out[...] = rows[pl.ds(pl.multiple_of(shifts[0] * WS, WS), out.shape[0]), :].astype(BF16)


def stack_rows(ids, shifts, got_o, got_e, fine, base):
    n_tok, width = fine.shape
    vmem = pl.BlockSpec(memory_space=pltpu.VMEM)
    smem = pl.BlockSpec(memory_space=pltpu.SMEM)
    return pl.pallas_call(
        lambda ids, shifts, *refs: stack_kernel(ids, shifts, base, *refs),
        in_specs=[smem, smem] + [vmem] * 3,
        out_specs=vmem,
        out_shape=jax.ShapeDtypeStruct((n_tok + n_tok // 2, width), BF16),
        scratch_shapes=[pltpu.VMEM((2 * n_tok, width), F32)],
        compiler_params=pltpu.CompilerParams(vmem_limit_bytes=VMEM_LIMIT),
        cost_estimate=COST_STACK,
        name="stack_rows",
    )(ids, shifts, got_o, got_e, fine)


def window_kernel(last, count, ids, shifts, left, mid, right, q, gain, w_k, w_v, *refs):
    weights, (out, lse), held = refs[:count], refs[count : count + 2], refs[count + 2 : 2 * count + 2]
    k_buf, v_buf, sems = refs[2 * count + 2 :]
    loads = [pltpu.make_async_copy(w_k, k_buf, sems.at[0]), pltpu.make_async_copy(w_v, v_buf, sems.at[1])]
    for copy in loads:
        copy.start()
    early = [
        pltpu.make_async_copy(w.at[0 : h.shape[0], 0 : h.shape[1]], h, sems.at[2 + i])
        for i, (w, h) in enumerate(zip(weights, held))
    ]
    span, width = left.shape
    strip, member = ids[0], ids[1]
    shift_row, shift_col = shifts[0], shifts[1]
    turn = lambda ref: pltpu.roll(ref[...].astype(F32).reshape(span // WS, WS, width), WS - shift_col, 1)
    a, b, c = turn(left), turn(mid), turn(right)
    stays = iota((1, WS, width), 1) < WS - shift_col
    fine = jnp.concatenate([jnp.where(stays, a, b), jnp.where(stays, b, c)], axis=0).reshape(2 * span, width)
    normed = rms(fine, gain[...]).astype(BF16)
    loads[0].wait()
    keys = jnp.dot(normed, k_buf[...], preferred_element_type=F32).astype(BF16)
    loads[1].wait()
    for copy in early:
        copy.start()
    values = jnp.dot(normed, v_buf[...], preferred_element_type=F32).astype(BF16)
    per = 2 * WS * WS
    shape = (128, 2 * per)
    query = lax.rem(iota(shape, 0), 64)
    column_q = lax.rem(query, WS)
    key = iota(shape, 1)
    block = lax.shift_right_arithmetic(key, 7)
    within = lax.bitwise_and(key, per - 1)
    column_k = block * WS - WS + shift_col + lax.bitwise_and(within, WS - 1)
    same_col = (column_q >= shift_col) == (block == 1)
    wrap_col = ((column_k < 0) & (member == 0)) | ((column_k >= WS) & (member == last[1]))
    low = iota((64, 128), 1) < HD
    lane = iota((64, 128), 1)
    own = (iota((128, 128), 0) < 64) == (iota((128, 128), 1) < HD)
    for half in range(2):
        row_q = WS * half + lax.shift_right_arithmetic(query, 3)
        line_k = WS * half + lax.shift_right_arithmetic(within, 3)
        row_k = line_k + shift_row - WS
        same_row = lax.shift_right_arithmetic(row_q - shift_row + WS, 3) == lax.shift_right_arithmetic(line_k, 3)
        wrap_row = ((row_k < 0) & (strip == 0)) | ((row_k >= 2 * WS) & (strip == last[0]))
        seen = same_row & same_col & jnp.logical_not(wrap_row | wrap_col)
        rows = slice(64 * half, 64 * half + 64)
        pick = lambda x: jnp.concatenate(
            [x[span * i + 64 * half : span * i + 64 * half + per] for i in range(2)], axis=0
        )
        keys_h, values_h = pick(keys), pick(values)
        marks = jnp.zeros((64, 128), F32)
        for pair in range(HEADS // 2):
            lanes = slice(128 * pair, 128 * pair + 128)
            q_pair = q[rows, lanes]
            q_both = jnp.concatenate([q_pair, q_pair], axis=0)
            q_both = jnp.where(own, q_both, jnp.zeros_like(q_both))
            score = lax.dot_general(
                q_both, keys_h[:, lanes], (((1,), (1,)), ((), ())), preferred_element_type=F32
            )
            score = jnp.where(seen, score, LOW)
            peak = jnp.max(score, axis=-1, keepdims=True)
            weight = jnp.exp(score - peak)
            total = jnp.sum(weight, axis=-1, keepdims=True)
            mixed = jnp.dot(weight.astype(BF16), values_h[:, lanes], preferred_element_type=F32) / total
            out[rows, lanes] = jnp.where(low, mixed[:64], mixed[64:])
            level = peak + jnp.log(total)
            marks = jnp.where(lane == 2 * pair, level[:64], marks)
            marks = jnp.where(lane == 2 * pair + 1, level[64:], marks)
        lse[rows, :] = marks
    for copy in early:
        copy.wait()


def window_attention(ids, shifts, left, mid, right, q, gain, w_k, w_v, weights, last):
    n_tok, width = q.shape
    count = len(weights)
    vmem = pl.BlockSpec(memory_space=pltpu.VMEM)
    smem = pl.BlockSpec(memory_space=pltpu.SMEM)
    return pl.pallas_call(
        lambda *refs: window_kernel(last, count, *refs),
        in_specs=[smem, smem] + [vmem] * 5 + [pl.BlockSpec(memory_space=pltpu.HBM)] * (2 + count),
        out_specs=[vmem] * (2 + count),
        out_shape=[
            jax.ShapeDtypeStruct((n_tok, width), F32),
            jax.ShapeDtypeStruct((n_tok, 128), F32),
        ]
        + [jax.ShapeDtypeStruct((min(w.shape[0], CHUNK), min(w.shape[1], CHUNK)), w.dtype) for w in weights],
        scratch_shapes=[
            pltpu.VMEM((width, width), BF16),
            pltpu.VMEM((width, width), BF16),
            pltpu.SemaphoreType.DMA((2 + count,)),
        ],
        compiler_params=pltpu.CompilerParams(vmem_limit_bytes=VMEM_LIMIT),
        cost_estimate=COST,
        name="window_attention",
    )(ids, shifts, left, mid, right, q, gain, w_k, w_v, *weights)


def attend(q, kv, kv_t):
    score = jnp.dot(kv, jnp.concatenate([q, jnp.zeros_like(q)], axis=0), preferred_element_type=F32)
    peak = jnp.max(score, axis=0, keepdims=True)
    weight = jnp.exp(score - peak)
    sums = jnp.sum(weight, axis=0, keepdims=True)
    mixed = jnp.dot(kv_t, weight.astype(BF16), preferred_element_type=F32)
    level = peak + jnp.log(sums)
    first = level.astype(BF16).astype(F32)
    second = (level - first).astype(BF16).astype(F32)
    third = level - first - second
    line = iota((16, q.shape[1]), 0)
    marks = jnp.where(line == 0, first, jnp.where(line == 1, second, jnp.where(line == 2, third, 0.0)))
    return jnp.concatenate([mixed[HD:] / sums, marks], axis=0)


def swap_halves(x):
    return pltpu.roll(x, 64, 1)


def top_rows(q_t, group):
    low = iota((1, 128), 1) < 64
    tiles = []
    for pair in range(4):
        a, b = (q_t[8 * group + 2 * pair + k].astype(F32) for k in range(2))
        tiles.append(jnp.where(low, a, swap_halves(b)).astype(BF16))
    return jnp.concatenate(tiles, axis=1)


def here_kernel(total, ids, table, q_t, own, got_o, got_e, out, store, turned):
    n_own = own.shape[0]
    per_strip = n_own // 128
    even = lax.rem(ids[0], 2) == 0
    blocked = lambda ref: ref[0:n_own, :].reshape(per_strip, 128, 128)
    above, below = blocked(got_o), blocked(got_e)
    store[0:per_strip] = jnp.where(even, above, below)
    store[per_strip : 2 * per_strip] = blocked(own)
    store[2 * per_strip :] = jnp.where(even, below, above)
    chosen = local_blocks(ids, table, per_strip, total)
    kv = jnp.concatenate([store[b] for b in chosen], axis=0)
    turned[...] = kv.astype(F32).T.astype(BF16)
    kv_t = turned[...]
    mixed = attend(jnp.concatenate([q_t[m] for m in range(q_t.shape[0])], axis=1), kv, kv_t)
    for m in range(q_t.shape[0]):
        out[m] = mixed[:, 128 * m : 128 * m + 128].astype(BF16)


def here_attention(ids, table, q_t, own, got_o, got_e, total):
    vmem = pl.BlockSpec(memory_space=pltpu.VMEM)
    smem = pl.BlockSpec(memory_space=pltpu.SMEM)
    members, _, n_tok = q_t.shape
    return pl.pallas_call(
        lambda *refs: here_kernel(total, *refs),
        in_specs=[smem, smem] + [vmem] * 4,
        out_specs=vmem,
        out_shape=jax.ShapeDtypeStruct((members, HD + 16, n_tok), BF16),
        scratch_shapes=[
            pltpu.VMEM((3 * own.shape[0] // 128, 128, 128), BF16),
            pltpu.VMEM((128, 128 * table.shape[1]), BF16),
        ],
        compiler_params=pltpu.CompilerParams(vmem_limit_bytes=VMEM_LIMIT),
        cost_estimate=COST_HERE,
        name="here_attention",
    )(ids, table, q_t, own, got_o, got_e)


def choose_kernel(after, ids, table, far_straight, far_handed, got_o, got_e, own, kv, kv_t, store):
    n_own = own.shape[0]
    per_strip = n_own // 128
    even = lax.rem(ids[0], 2) == 0
    blocked = lambda ref: ref[0:n_own, :].reshape(per_strip, 128, 128)
    handed = lax.rem(ids[0], PLANE) == 1
    store[0:per_strip] = jnp.where(handed, blocked(far_handed), blocked(far_straight))
    store[per_strip : 2 * per_strip] = jnp.where(even, blocked(got_o), blocked(got_e))
    store[2 * per_strip :] = blocked(own)
    for i in range(table.shape[0]):
        block = store[table[i]]
        at = slice(128 * i, 128 * i + 128)
        kv[at, :] = block
        kv_t[:, at] = block.astype(F32).T.astype(BF16)


def choose_blocks(after, ids, table, far_straight, far_handed, got_o, got_e, own):
    vmem = pl.BlockSpec(memory_space=pltpu.VMEM)
    smem = pl.BlockSpec(memory_space=pltpu.SMEM)
    keys = 128 * table.shape[0]
    return pl.pallas_call(
        choose_kernel,
        in_specs=[pl.BlockSpec(memory_space=pl.ANY), smem, smem] + [vmem] * 5,
        out_specs=[vmem] * 2,
        out_shape=[jax.ShapeDtypeStruct((keys, 128), BF16), jax.ShapeDtypeStruct((128, keys), BF16)],
        scratch_shapes=[pltpu.VMEM((3 * own.shape[0] // 128, 128, 128), BF16)],
        compiler_params=pltpu.CompilerParams(vmem_limit_bytes=VMEM_LIMIT),
        cost_estimate=COST_CHOOSE,
        name="choose_blocks",
    )(after, ids, table, far_straight, far_handed, got_o, got_e, own)


def before_kernel(after, after_too, shifts, q_t, kv, kv_t, here, out):
    lane = iota((1, 128), 1)
    earlier = lane < WS * shifts[0]
    for group in range(q_t.shape[0] // 8):
        top = attend(top_rows(q_t, group), kv[...], kv_t[...])
        for pair in range(4):
            t = top[:, 128 * pair : 128 * pair + 128]
            for k in range(2):
                m = 8 * group + 2 * pair + k
                mine = t if k == 0 else swap_halves(t)
                out[m] = jnp.where(earlier, mine, here[m].astype(F32)).astype(BF16)


def before_attention(after, after_too, shifts, q_t, kv, kv_t, here):
    vmem = pl.BlockSpec(memory_space=pltpu.VMEM)
    return pl.pallas_call(
        before_kernel,
        in_specs=[pl.BlockSpec(memory_space=pl.ANY)] * 2 + [pl.BlockSpec(memory_space=pltpu.SMEM)] + [vmem] * 4,
        out_specs=vmem,
        out_shape=jax.ShapeDtypeStruct(here.shape, BF16),
        compiler_params=pltpu.CompilerParams(vmem_limit_bytes=VMEM_LIMIT),
        cost_estimate=COST,
        name="before_attention",
    )(after, after_too, shifts, q_t, kv, kv_t, here)


def finish_kernel(
    fine, near, near_lse, coarse, gain, w_out, gate_0, up_0, down_0, w_gate, w_up, w_down, out, g_buf, u_buf, d_buf, sems
):
    steps = w_gate.shape[1] // CHUNK
    loads = []
    for i in range(1, steps):
        at = pl.ds(CHUNK * i, CHUNK)
        loads.append(
            [
                pltpu.make_async_copy(w_gate.at[:, at], g_buf.at[i - 1], sems.at[3 * i - 3]),
                pltpu.make_async_copy(w_up.at[:, at], u_buf.at[i - 1], sems.at[3 * i - 2]),
                pltpu.make_async_copy(w_down.at[at], d_buf.at[i - 1], sems.at[3 * i - 1]),
            ]
        )
    for group in loads:
        for copy in group:
            copy.start()
    heads = coarse.shape[0]
    far = jnp.concatenate([coarse[h, 0:HD, :].astype(F32) for h in range(heads)], axis=0).T
    marks = [coarse[h, HD : HD + 16, :].astype(F32) for h in range(heads)]
    level = jnp.concatenate([m[0:1] + m[1:2] + m[2:3] for m in marks], axis=0).T
    diff = near_lse[:, 0:heads] - level
    share = 1.0 / (1.0 + jnp.exp(diff))
    share = jnp.concatenate(
        [jnp.broadcast_to(share[:, h : h + 1], (share.shape[0], HD)) for h in range(heads)], axis=1
    )
    head_out = (near[...] * (1.0 - share) + far * share).astype(BF16)
    mid = fine[...].astype(F32) + jnp.dot(head_out, w_out[...], preferred_element_type=F32)
    normed = rms(mid, gain[...]).astype(BF16)
    total = mid
    for i in range(steps):
        if i == 0:
            parts = (gate_0, up_0, down_0)
        else:
            for copy in loads[i - 1]:
                copy.wait()
            parts = (g_buf.at[i - 1], u_buf.at[i - 1], d_buf.at[i - 1])
        gate = jnp.dot(normed, parts[0][...], preferred_element_type=F32)
        up = jnp.dot(normed, parts[1][...], preferred_element_type=F32)
        hidden = (gate * (1.0 / (1.0 + jnp.exp(-gate))) * up).astype(BF16)
        total = total + jnp.dot(hidden, parts[2][...], preferred_element_type=F32)
    out[...] = total.astype(BF16)


def finish(fine, near, near_lse, coarse, gain, w_out, gate_0, up_0, down_0, w_gate, w_up, w_down):
    n_tok, width = fine.shape
    rest = w_gate.shape[1] // CHUNK - 1
    vmem = pl.BlockSpec(memory_space=pltpu.VMEM)
    hbm = pl.BlockSpec(memory_space=pltpu.HBM)
    return pl.pallas_call(
        finish_kernel,
        in_specs=[vmem] * 9 + [hbm] * 3,
        out_specs=vmem,
        out_shape=jax.ShapeDtypeStruct((n_tok, width), BF16),
        scratch_shapes=[
            pltpu.VMEM((rest, width, CHUNK), BF16),
            pltpu.VMEM((rest, width, CHUNK), BF16),
            pltpu.VMEM((rest, CHUNK, width), BF16),
            pltpu.SemaphoreType.DMA((3 * rest,)),
        ],
        compiler_params=pltpu.CompilerParams(vmem_limit_bytes=VMEM_LIMIT),
        cost_estimate=COST,
        name="finish",
    )(fine, near, near_lse, coarse, gain, w_out, gate_0, up_0, down_0, w_gate, w_up, w_down)


def local(
    fine,
    coarse,
    block_table,
    shifts,
    attn_gain,
    w_query,
    w_key,
    w_value,
    w_out,
    coarse_key,
    coarse_value,
    mlp_gain,
    w_gate,
    w_up,
    w_down,
):
    strips = lax.axis_size("tile")
    members = lax.axis_size("narrow")
    strip = lax.axis_index("tile").astype(jnp.int32)
    member = lax.axis_index("narrow").astype(jnp.int32)
    ids = jnp.stack([strip, member])
    rows, columns, width = fine.shape
    blocks, block_tokens, cw = coarse.shape
    total = blocks * strips
    n_own = blocks * block_tokens
    flat = fine.reshape(rows * columns, width)
    table = block_table
    gain = attn_gain.reshape(1, width)

    stay = lambda x: pltpu.with_memory_space_constraint(x, pltpu.HBM)
    flat_hbm = stay(flat)
    kv, pay_o, pay_e = project(
        ids, stay(table), stay(coarse.reshape(n_own, cw)), stay(coarse_key), stay(coarse_value), flat_hbm, total
    )
    odd_pairs = [(i, (i - 1) % strips if i % 2 == 0 else (i + 1) % strips) for i in range(strips)]
    even_pairs = [(i, i ^ 1) for i in range(strips)]
    got_o = lax.ppermute(pay_o, "tile", odd_pairs)
    got_e = lax.ppermute(pay_e, "tile", even_pairs)
    far_straight = lax.ppermute(
        kv, "tile", [(i, (i + 2) % strips) for i in range(strips) if i % PLANE != PLANE - 1]
    )
    q, q_t = queries(kv, flat_hbm, gain, stay(w_query))
    q_head = lax.all_to_all(q_t, "narrow", 0, 0, tiled=True)

    far_handed = lax.ppermute(got_o, "tile", [(i, i + 1) for i in range(0, strips, PLANE)])
    mark_row = n_own + HALO * WS * (width // 128)
    table_before = jnp.where(strip % 2 == 0, got_o[mark_row, :8], got_e[mark_row, :8]).astype(jnp.int32)

    stacked = stack_rows(ids, shifts, got_o, got_e, flat, n_own)
    stacked, table_before = lax.optimization_barrier((stacked, table_before))
    right_of = lax.ppermute(stacked, "narrow", [(i, i - 1) for i in range(1, members)])
    left_of = lax.ppermute(stacked, "narrow", [(i, i + 1) for i in range(members - 1)])
    here = here_attention(ids, table, q_head, kv, got_o, got_e, total)
    kv_before, kv_before_t = choose_blocks(here, ids, table_before, far_straight, far_handed, got_o, got_e, kv)
    from_coarse = before_attention(left_of, right_of, shifts, q_head, kv_before, kv_before_t, here)
    from_coarse = lax.all_to_all(from_coarse, "narrow", 0, 0, tiled=True)
    near, near_lse, *held = window_attention(
        ids,
        shifts,
        left_of,
        stacked,
        right_of,
        q,
        gain,
        stay(w_key),
        stay(w_value),
        (stay(w_out), stay(w_gate), stay(w_up), stay(w_down)),
        (strips - 1, members - 1),
    )
    out = finish(
        flat,
        near,
        near_lse,
        from_coarse,
        mlp_gain.reshape(1, width),
        *held,
        stay(w_gate),
        stay(w_up),
        stay(w_down),
    )
    return out.reshape(rows, columns, width)


def solution(mesh):
    placed = (
        P("tile", "narrow", None),
        P("tile", None, None),
        P("tile", None),
    ) + (P(),) * 12
    return jax.shard_map(
        local, mesh=mesh, in_specs=placed, out_specs=P("tile", "narrow", None), check_vma=False
    )
```
